128 devices in a mesh: seq: 8 (over z, core), exp: 16 (over x, y).
Axes of the slice: x: 4, y: 4, z: 4, core: 2. Of those that a mesh axis runs over, the one named last changes fastest.
Arguments:
- mixer_in: bfloat16 [16, 1024, 2048], P('exp', 'seq'), may hold values from -6 to 6
- bc: bfloat16 [16, 1024, 32], P('exp', 'seq'), may hold values from -0.59765625 to 0.59765625
- log_decay: float32 [16, 1024, 32], P('exp', 'seq'), may hold values from -2 to 0
- skip_gain: float32 [32], replicated, may hold values from 0.1 to 1.9
- norm_gain: bfloat16 [2048], replicated, may hold values from 0.099609375 to 1.8984375
- routes: int32 [16, 1024, 2], P('exp', 'seq'), may hold values from 0 to 15, all different within a row; in each aligned block of 128 rows (0 to 127, 128 to 255, ..., all dimensions but the last counted through in order) at most 20 rows name the same one
- route_weight: float32 [16, 1024, 2], P('exp', 'seq'), may hold values from 0.2 to 1
- w_gate: bfloat16 [16, 2048, 7168], P('exp', None, 'seq'), may hold values from -0.125 to 0.125
- w_up: bfloat16 [16, 2048, 7168], P('exp', None, 'seq'), may hold values from -0.125 to 0.125
- w_down: bfloat16 [16, 7168, 2048], P('exp', 'seq'), may hold values from -0.0625 to 0.0625
- saved_pre: bfloat16 [16, 2, 2560, 7168], P('exp', None, None, 'seq'), may hold values from -6 to 6
- d_out: bfloat16 [16, 1024, 2048], P('exp', 'seq'), may hold values from -6 to 6
Outputs:
- residual: bfloat16 [16, 1024, 2048], P('exp', 'seq')
- grad_in: bfloat16 [16, 1024, 2048], P('exp', 'seq')
The draws below stay inside these ranges and needn't reach their ends.
Inputs may be any that keep to these rules, and one draw needn't show every extreme that they name: `routes`: in each block of 128 positions of one sequence no expert is named more than 20 times, and some block names some expert exactly 20 times.
All inputs are finite; a program needn't handle non-finite values.
Results may differ from the reference program's by a relative error of at most 0.0075.
Values may be sent and summed in bfloat16 or wider, within the bound.
No kernel may reach another device: no remote copies, remote signals or barrier semaphores. Data moves between devices by JAX's collectives and lax.ppermute only.
A program may use at most 192 MiB of HBM per device.

```python
import math
import jax
import jax.numpy as jnp
import numpy as np
from jax import lax

D = 2048
FF = 7168
STATE = 16
HEAD = 64
SPAN = 128
TOP = 2
TOK_DEV = 128
EXPERTS = 16
HEADS = 32
BATCH_SEQUENCES = 16
SEQUENCE_LENGTH = 1024
SOURCES = 128
CAP = 20
N_SEQ = 8
N_EXP = 16


def draw_log_decay(key, part):
    key = jax.random.fold_in(key, 11)
    split_random_keys = jax.random.split(key, 7)
    fast_share = 0.5
    spread_log = 0.5
    fast_heads = jax.random.uniform(split_random_keys[0], (BATCH_SEQUENCES, 1, HEADS)) < fast_share
    fast_rate = jax.random.uniform(split_random_keys[1], (BATCH_SEQUENCES, 1, HEADS), minval=1.0 / 50.0, maxval=1.0 / 30.0)
    slow_rate = jax.random.uniform(split_random_keys[2], (BATCH_SEQUENCES, 1, HEADS), minval=0.05, maxval=0.25) / SEQUENCE_LENGTH
    baseline_rate = jnp.where(fast_heads, fast_rate, slow_rate)
    blocks = SEQUENCE_LENGTH // TOK_DEV
    scale_per_block = jnp.exp(jax.random.uniform(split_random_keys[3], (BATCH_SEQUENCES, blocks, 1, HEADS), minval=-0.69, maxval=0.69))
    scale_per_block = jnp.broadcast_to(scale_per_block, (BATCH_SEQUENCES, blocks, TOK_DEV, HEADS)).reshape(BATCH_SEQUENCES, SEQUENCE_LENGTH, HEADS)
    random_wobble = jnp.exp(jax.random.uniform(split_random_keys[4], (BATCH_SEQUENCES, SEQUENCE_LENGTH, HEADS), minval=-spread_log, maxval=spread_log))
    spike_events = jax.random.randint(split_random_keys[5], (BATCH_SEQUENCES, 2), 0, SEQUENCE_LENGTH)
    position_indices = jnp.arange(SEQUENCE_LENGTH)
    spike_positions = jnp.sum((position_indices[None, :, None] == spike_events[:, None, :]).astype(jnp.float32), axis=2)
    spike_decay_drop = jnp.log(jax.random.uniform(split_random_keys[6], (BATCH_SEQUENCES, SEQUENCE_LENGTH, 1), minval=0.5, maxval=0.8))
    return -baseline_rate * scale_per_block * random_wobble + spike_positions[:, :, None] * spike_decay_drop


def block_scale(key, extent, cuts, low, largest):
    gain, own = 1.0, jax.random.fold_in(key, 6)
    for position, blocks in cuts:
        heights = jnp.exp(jax.random.uniform(jax.random.fold_in(own, position), (blocks,), jnp.float32, low / len(cuts), largest / len(cuts)))
        gain = gain * jnp.repeat(heights, extent[position] // blocks).reshape([-1 if axis == position else 1 for axis in range(len(extent))])
    return gain


def routed_block(rng, own, number, rows, count, top, most, slope):
    ranking = jax.random.permutation(rng, count)
    crowded, ordinary = load_shares(count, rows * top, most, slope, True), load_shares(count, rows * top, most, slope, False)
    places = jnp.arange(count)

    def named(lengths, offset_by):
        used = int((lengths > 0).sum())
        fixed = max(1, used // 4)
        passed = fixed + (places - fixed + offset_by * (used - fixed)) % max(1, count - fixed)
        return jnp.zeros((count,), jnp.int32).at[ranking[jnp.where(places < fixed, places, passed)]].set(jnp.asarray(lengths, jnp.int32))

    lengths = jnp.where(number % 4 == 0, named(crowded, number // 4), named(ordinary, number - number // 4 - 1))
    mixed = jax.random.permutation(jax.random.fold_in(own, 3), count)
    giver, sink = mixed[0:count // 2 * 2:2], mixed[1:count // 2 * 2:2]
    slack = jnp.minimum(lengths[giver] - 1, most - lengths[sink]) // 2
    slack = jnp.where((giver == ranking[0]) | (sink == ranking[0]) | (lengths[sink] == 0), 0, jnp.maximum(slack, 0))
    passed = jax.random.randint(jax.random.fold_in(own, 4), (count // 2,), 0, 1 << 20) % (slack + 1)
    lengths = lengths.at[giver].add(-passed).at[sink].add(passed)
    members = jnp.searchsorted(jnp.cumsum(lengths), jnp.arange(rows * top), side="right").astype(jnp.int32)
    table = members.reshape(top, rows).T
    table = table[jax.random.permutation(jax.random.fold_in(own, 1), rows)]
    offset_by = jax.random.randint(jax.random.fold_in(own, 2), (rows, 1), 0, top)
    return jnp.take_along_axis(table, (jnp.arange(top)[None, :] + offset_by) % top, axis=1)


def load_shares(count, total, most, lean, full):
    loads = [(1 << 20) // math.isqrt(standing ** lean) + 1 for standing in range(1, count + 1)]
    largest = most if full else min(most, max(-(-total // count), total * loads[0] // sum(loads)))
    least = 1 if total - largest >= count - 1 else 0
    holding, spare = [largest] + [least] * (count - 1), total - largest - least * (count - 1)
    while spare > 0:
        candidates = [i for i in range(1, count) if holding[i] < largest] or [i for i in range(1, count) if holding[i] < most]
        whole, budget = sum([loads[i] for i in candidates]), spare
        for i in candidates:
            more = min(most - holding[i], max(1, budget * loads[i] // whole), spare)
            holding[i] = holding[i] + more
            spare = spare - more
    return np.array(holding)


def noise(rng, dims, scale, reach, shards=(), kind=jnp.bfloat16):
    values = scale * jax.random.normal(rng, dims, jnp.float32)
    if shards:
        values = values * block_scale(rng, dims, shards, -0.22, 0.18)
    return jnp.clip(values, -reach, reach).astype(kind)


def setup_inputs(seed: int = 0) -> dict:
    keys = jax.random.split(jax.random.key(seed), 13)
    mixer_in = noise(keys[0], (BATCH_SEQUENCES, SEQUENCE_LENGTH, D), 1.0, 6.0, ((0, 16), (1, 8)))
    bc = noise(keys[1], (BATCH_SEQUENCES, SEQUENCE_LENGTH, 2 * STATE), 0.09, 0.59765625, ((0, 16), (1, 8)))
    log_decay = draw_log_decay(jax.random.fold_in(keys[12], 71), 0)
    skip_gain = jnp.clip(1.0 + 0.18 * jax.random.normal(keys[3], (HEADS,), jnp.float32), 0.1, 1.9)
    norm_gain = jnp.clip(1.0 + 0.18 * jax.random.normal(keys[4], (D,), jnp.float32), 0.099609375, 1.8984375).astype(jnp.bfloat16)
    routes_keys = jax.random.split(jax.random.fold_in(keys[5], 1), BATCH_SEQUENCES * SEQUENCE_LENGTH // TOK_DEV)
    routes_turns = jax.random.permutation(jax.random.fold_in(keys[5], 3), BATCH_SEQUENCES * SEQUENCE_LENGTH // TOK_DEV)
    routes = jax.vmap(lambda own, number: routed_block(jax.random.fold_in(keys[5], 2), own, number, TOK_DEV, EXPERTS, TOP, CAP, 2))(routes_keys, routes_turns).reshape((BATCH_SEQUENCES, SEQUENCE_LENGTH, TOP))
    route_weight = jnp.clip(0.2 + 0.8 * jax.random.uniform(keys[6], (BATCH_SEQUENCES, SEQUENCE_LENGTH, TOP), jnp.float32) ** block_scale(keys[6], (BATCH_SEQUENCES, SEQUENCE_LENGTH, TOP), ((0, 16), (1, 8)), -0.2, 0.2), 0.2, 1.0)
    w_gate = noise(keys[7], (EXPERTS, D, FF), D ** -0.5, 0.125, ((0, 16), (2, 8)))
    w_up = noise(keys[8], (EXPERTS, D, FF), D ** -0.5, 0.125, ((0, 16), (2, 8)))
    w_down = noise(keys[9], (EXPERTS, FF, D), FF ** -0.5, 0.0625, ((0, 16), (1, 8)))
    saved_pre = noise(keys[10], (EXPERTS, 2, SOURCES * CAP, FF), 1.0, 6.0, ((0, 16), (3, 8)))
    d_out = noise(keys[11], (BATCH_SEQUENCES, SEQUENCE_LENGTH, D), 1.0, 6.0, ((0, 16), (1, 8)))
    return {"mixer_in": mixer_in, "bc": bc, "log_decay": log_decay, "skip_gain": skip_gain, "norm_gain": norm_gain, "routes": routes, "route_weight": route_weight, "w_gate": w_gate, "w_up": w_up, "w_down": w_down, "saved_pre": saved_pre, "d_out": d_out}


HIGHEST = lax.Precision.HIGHEST
EPSILON = 1e-05

def decay_mask(log_rates):
    cum_log = jnp.cumsum(log_rates, axis=0)
    position_indices = jnp.arange(log_rates.shape[0], dtype=jnp.int32)
    causal = (position_indices[:, None] >= position_indices[None, :])[:, :, None]
    log_gaps = cum_log[:, None, :] - cum_log[None, :, :]
    return (cum_log, jnp.where(causal, jnp.exp(jnp.minimum(log_gaps, 0.0)), 0.0))

def span_forward(state_now, pieces):
    values, write_rows, read_rows, log_rates, write_raw, read_raw = pieces
    cum_log, mask_table = decay_mask(log_rates)
    scores = jnp.dot(read_raw, write_raw.T, preferred_element_type=jnp.float32)
    weights = mask_table * scores[:, :, None]
    result = jnp.einsum('tsh,shp->thp', weights, values, precision=HIGHEST)
    carried = jnp.einsum('tn,nhp->thp', read_rows, state_now, precision=HIGHEST)
    result = result + jnp.exp(cum_log)[:, :, None] * carried
    to_end = jnp.exp(cum_log[-1][None, :] - cum_log)
    added = jnp.einsum('sn,shp->nhp', write_rows, to_end[:, :, None] * values, precision=HIGHEST)
    return (jnp.exp(cum_log[-1])[None, :, None] * state_now + added, result)

def span_backward(adjoint, pieces):
    gradient, write_rows, read_rows, log_rates, write_raw, read_raw = pieces
    cum_log, mask_table = decay_mask(log_rates)
    scores = jnp.dot(read_raw, write_raw.T, preferred_element_type=jnp.float32)
    weights = mask_table * scores[:, :, None]
    result = jnp.einsum('tsh,thp->shp', weights, gradient, precision=HIGHEST)
    to_end = jnp.exp(cum_log[-1][None, :] - cum_log)
    carried = jnp.einsum('sn,nhp->shp', write_rows, adjoint, precision=HIGHEST)
    result = result + to_end[:, :, None] * carried
    added = jnp.einsum('tn,thp->nhp', read_rows, jnp.exp(cum_log)[:, :, None] * gradient, precision=HIGHEST)
    return (jnp.exp(cum_log[-1])[None, :, None] * adjoint + added, result)

def local_pass(step_fn, values, write_rows, read_rows, log_rates, write_raw, read_raw, backwards):
    spans = values.shape[0] // SPAN
    head_count = values.shape[1]
    head_size = values.shape[2]
    state_size = write_rows.shape[1]
    pieces = (values.reshape(spans, SPAN, head_count, head_size), write_rows.reshape(spans, SPAN, state_size), read_rows.reshape(spans, SPAN, state_size), log_rates.reshape(spans, SPAN, head_count), write_raw.reshape(spans, SPAN, state_size), read_raw.reshape(spans, SPAN, state_size))
    start_state = jnp.zeros((state_size, head_count, head_size), jnp.float32)
    end_state, outputs = lax.scan(step_fn, start_state, pieces, reverse=backwards)
    return (outputs.reshape(values.shape), end_state)

def slice_grad(row_block, saved_rows, gate_rows, up_rows, down_rows):
    hidden_grad = jnp.dot(row_block, down_rows.T, preferred_element_type=jnp.float32)
    gate_pre = saved_rows[0].astype(jnp.float32)
    up_pre = saved_rows[1].astype(jnp.float32)
    sigmoid_g = jax.nn.sigmoid(gate_pre)
    gate_grad = (hidden_grad * up_pre * sigmoid_g * (1.0 + gate_pre * (1.0 - sigmoid_g))).astype(jnp.bfloat16)
    up_grad = (hidden_grad * gate_pre * sigmoid_g).astype(jnp.bfloat16)
    return jnp.dot(gate_grad, gate_rows.T, preferred_element_type=jnp.float32) + jnp.dot(up_grad, up_rows.T, preferred_element_type=jnp.float32)

def to_blocks(array):
    rest = array.shape[2:]
    moved = jnp.transpose(array.reshape((BATCH_SEQUENCES, N_SEQ, TOK_DEV) + rest), (1, 0, 2) + tuple(range(3, 3 + len(rest))))
    return moved.reshape((N_SEQ * N_EXP, TOK_DEV) + rest)

def reference(mixer_in, bc, log_decay, skip_gain, norm_gain, routes, route_weight, w_gate, w_up, w_down, saved_pre, d_out):
    values = mixer_in.astype(jnp.float32).reshape(BATCH_SEQUENCES, SEQUENCE_LENGTH, HEADS, HEAD)
    write_raw = bc[:, :, :STATE]
    read_raw = bc[:, :, STATE:]
    write_rows = write_raw.astype(jnp.float32)
    read_rows = read_raw.astype(jnp.float32)

    def forward_one(vals, writes, reads, rates, writes_raw, reads_raw):
        return local_pass(span_forward, vals, writes, reads, rates, writes_raw, reads_raw, False)[0]
    mixer_out = jax.vmap(forward_one)(values, write_rows, read_rows, log_decay, write_raw, read_raw)
    mixer_out = mixer_out + skip_gain[None, None, :, None] * values
    residual = (mixer_in.astype(jnp.float32) + mixer_out.reshape(BATCH_SEQUENCES, SEQUENCE_LENGTH, D)).astype(jnp.bfloat16)
    sources = N_SEQ * N_EXP
    route_rows = to_blocks(routes).reshape(sources, TOK_DEV * TOP)
    onehot = (route_rows[:, :, None] == jnp.arange(EXPERTS, dtype=jnp.int32)[None, None, :]).astype(jnp.int32)
    before = (jnp.cumsum(onehot, axis=1).astype(jnp.int32) - onehot).astype(jnp.int32)
    slot_index = lax.optimization_barrier(jnp.sum(before * onehot, axis=2)).astype(jnp.int32)
    source_ids = jnp.arange(sources, dtype=jnp.int32)[:, None]
    location = ((route_rows * sources + source_ids) * CAP + slot_index).astype(jnp.int32).reshape(-1)
    grad_rows = jnp.repeat(to_blocks(d_out), TOP, axis=1).reshape(-1, D)
    buffer = jnp.zeros((EXPERTS * sources * CAP, D), jnp.bfloat16).at[location].set(grad_rows)

    def expert_grad(operands):
        row_block, saved_rows, gate_rows, up_rows, down_rows = operands
        slice_width = FF // N_SEQ
        summed = jnp.zeros(row_block.shape, jnp.float32)
        for piece_index in range(N_SEQ):
            lower_end = piece_index * slice_width
            upper_end = lower_end + slice_width
            partial_value = slice_grad(row_block, saved_rows[:, :, lower_end:upper_end], gate_rows[:, lower_end:upper_end], up_rows[:, lower_end:upper_end], down_rows[lower_end:upper_end, :])
            rounded = lax.optimization_barrier(partial_value.astype(jnp.bfloat16))
            summed = summed + rounded.astype(jnp.float32)
        return summed
    slot_grads = lax.map(expert_grad, (buffer.reshape(EXPERTS, sources * CAP, D), saved_pre, w_gate, w_up, w_down))
    pair_grad = slot_grads.reshape(-1, D)[location].reshape(sources, TOK_DEV, TOP, D)
    weight_rows = to_blocks(route_weight)
    moe_blocks = lax.optimization_barrier(jnp.sum(pair_grad * weight_rows[:, :, :, None], axis=2))
    moe_grad = jnp.transpose(moe_blocks.reshape(N_SEQ, BATCH_SEQUENCES, TOK_DEV, D), (1, 0, 2, 3)).reshape(BATCH_SEQUENCES, SEQUENCE_LENGTH, D)
    resid_float = residual.astype(jnp.float32)
    root_mean = jnp.sqrt(lax.optimization_barrier(jnp.mean(resid_float * resid_float, axis=-1, keepdims=True)) + EPSILON)
    normed = resid_float / root_mean
    scaled = moe_grad * norm_gain.astype(jnp.float32)
    resid_grad = d_out.astype(jnp.float32) + (scaled - normed * lax.optimization_barrier(jnp.mean(scaled * normed, axis=-1, keepdims=True))) / root_mean

    def backward_one(grads, writes, reads, rates, writes_raw, reads_raw):
        return local_pass(span_backward, grads, writes, reads, rates, writes_raw, reads_raw, True)[0]
    gradient = resid_grad.reshape(BATCH_SEQUENCES, SEQUENCE_LENGTH, HEADS, HEAD)
    backward = jax.vmap(backward_one)(gradient, write_rows, read_rows, log_decay, write_raw, read_raw)
    backward = backward + skip_gain[None, None, :, None] * gradient
    grad_in = (resid_grad + backward.reshape(BATCH_SEQUENCES, SEQUENCE_LENGTH, D)).astype(jnp.bfloat16)
    return (residual, grad_in)
```

```python
import functools

import jax
import jax.numpy as jnp
from jax import lax
from jax.experimental import pallas as pl
from jax.experimental.pallas import tpu as pltpu
from jax.sharding import PartitionSpec as P

SPAN = 128
HEAD = 64


HIGHEST = lax.Precision.HIGHEST
EPSILON = 1e-05


def chip_shift(value, by):
    chips = lax.axis_size("seq") // 2
    pairs = [(2 * z + c, 2 * ((z + by) % chips) + c) for z in range(chips) for c in range(2)]
    return lax.ppermute(value, "seq", pairs)


def core_swap(value):
    return lax.ppermute(value, "seq", [(i, i ^ 1) for i in range(lax.axis_size("seq"))])


def added(*terms):
    total = terms[0].astype(jnp.float32)
    for term in terms[1:]:
        total = total + term.astype(jnp.float32)
    return total


def decay_mask(log_rates):
    cum_log = jnp.cumsum(log_rates, axis=0)
    position_indices = jnp.arange(log_rates.shape[0], dtype=jnp.int32)
    causal = (position_indices[:, None] >= position_indices[None, :])[:, :, None]
    log_gaps = cum_log[:, None, :] - cum_log[None, :, :]
    return (cum_log, jnp.where(causal, jnp.exp(jnp.minimum(log_gaps, 0.0)), 0.0))


def span_forward(state_now, pieces):
    values, write_rows, read_rows, log_rates, write_raw, read_raw = pieces
    cum_log, mask_table = decay_mask(log_rates)
    scores = jnp.dot(read_raw, write_raw.T, preferred_element_type=jnp.float32)
    weights = mask_table * scores[:, :, None]
    result = jnp.einsum("tsh,shp->thp", weights, values, precision=HIGHEST)
    carried = jnp.einsum("tn,nhp->thp", read_rows, state_now, precision=HIGHEST)
    result = result + jnp.exp(cum_log)[:, :, None] * carried
    to_end = jnp.exp(cum_log[-1][None, :] - cum_log)
    added = jnp.einsum("sn,shp->nhp", write_rows, to_end[:, :, None] * values, precision=HIGHEST)
    return (jnp.exp(cum_log[-1])[None, :, None] * state_now + added, result)


def span_backward(adjoint, pieces):
    gradient, write_rows, read_rows, log_rates, write_raw, read_raw = pieces
    cum_log, mask_table = decay_mask(log_rates)
    scores = jnp.dot(read_raw, write_raw.T, preferred_element_type=jnp.float32)
    weights = mask_table * scores[:, :, None]
    result = jnp.einsum("tsh,thp->shp", weights, gradient, precision=HIGHEST)
    to_end = jnp.exp(cum_log[-1][None, :] - cum_log)
    carried = jnp.einsum("sn,nhp->shp", write_rows, adjoint, precision=HIGHEST)
    result = result + to_end[:, :, None] * carried
    added = jnp.einsum(
        "tn,thp->nhp", read_rows, jnp.exp(cum_log)[:, :, None] * gradient, precision=HIGHEST
    )
    return (jnp.exp(cum_log[-1])[None, :, None] * adjoint + added, result)


def local_pass(step_fn, values, write_rows, read_rows, log_rates, write_raw, read_raw, backwards):
    spans = values.shape[0] // SPAN
    head_count = values.shape[1]
    head_size = values.shape[2]
    state_size = write_rows.shape[1]
    pieces = (
        values.reshape(spans, SPAN, head_count, head_size),
        write_rows.reshape(spans, SPAN, state_size),
        read_rows.reshape(spans, SPAN, state_size),
        log_rates.reshape(spans, SPAN, head_count),
        write_raw.reshape(spans, SPAN, state_size),
        read_raw.reshape(spans, SPAN, state_size),
    )
    start_state = jnp.zeros((state_size, head_count, head_size), jnp.float32)
    end_state, outputs = lax.scan(step_fn, start_state, pieces, reverse=backwards)
    return (outputs.reshape(values.shape), end_state)


def expert_kernel(counts, blocks, *refs):
    steps = len(counts)
    pieces, refs = refs[: sum(counts)], refs[sum(counts) :]
    saved, gate, up, down = refs[:4]
    outs, refs = refs[4 : 4 + steps], refs[4 + steps :]
    x, pre, w_gate, w_up, w_down, mixed, out, sem_x, sem_pre, sem_w, sem_out = refs
    rows = x.shape[1]
    units = w_down.shape[0]
    width = x.shape[2]
    loads = []
    taken = 0
    for step, count in enumerate(counts):
        parts = []
        below = 0
        for piece in pieces[taken : taken + count]:
            part = piece.shape[0]
            parts.append(
                pltpu.make_async_copy(
                    piece, x.at[step, pl.ds(below, part)], sem_x.at[taken + len(parts)]
                )
            )
            below += part
        taken += count
        start = pl.multiple_of(blocks[step] * rows, rows)
        before = pltpu.make_async_copy(
            saved.at[0, :, pl.ds(start, rows)], pre.at[step], sem_pre.at[step]
        )
        loads.append((parts, before))
    take_down = pltpu.make_async_copy(down, w_down, sem_w.at[0])
    take_gate = pltpu.make_async_copy(gate, w_gate, sem_w.at[1])
    take_up = pltpu.make_async_copy(up, w_up, sem_w.at[2])
    for part in loads[0][0]:
        part.start()
    take_down.start()
    loads[0][1].start()
    take_gate.start()
    take_up.start()
    for parts, before in loads[1:]:
        for part in parts:
            part.start()
        before.start()
    stores = []
    for step in range(steps):
        for part in loads[step][0]:
            part.wait()
        if step == 0:
            take_down.wait()
        loads[step][1].wait()
        for low in range(0, units, 256):
            high = min(low + 256, units)
            hidden = lax.dot_general(
                x[step], w_down[low:high], (((1,), (1,)), ((), ())),
                preferred_element_type=jnp.float32,
            )
            gate_pre = pre[step, 0, :, low:high].astype(jnp.float32)
            up_pre = pre[step, 1, :, low:high].astype(jnp.float32)
            sigma = 1.0 / (1.0 + jnp.exp(-gate_pre))
            scaled = hidden * sigma
            mixed[:, low:high] = (scaled * up_pre * (1.0 + gate_pre * (1.0 - sigma))).astype(
                jnp.bfloat16
            )
            mixed[:, units + low : units + high] = (scaled * gate_pre).astype(jnp.bfloat16)
        if step == 0:
            take_gate.wait()
            take_up.wait()
        slot = step % 2
        if step >= 2:
            stores[step - 2].wait()

        @pl.loop(0, width // 512)
        def columns(tile):
            low = pl.multiple_of(tile * 512, 512)
            weights = jnp.concatenate(
                [w_gate[pl.ds(low, 512)], w_up[pl.ds(low, 512)]], axis=1
            )
            out[slot, :, pl.ds(low, 512)] = lax.dot_general(
                mixed[...], weights, (((1,), (1,)), ((), ())),
                preferred_element_type=jnp.float32,
            ).astype(jnp.bfloat16)

        store = pltpu.make_async_copy(out.at[slot], outs[step], sem_out.at[step])
        store.start()
        stores.append(store)
    for store in stores[-2:]:
        store.wait()


def expert_rows(blocks, pieces, saved, gate, up, down):
    steps = len(pieces)
    counts = tuple(len(parts) for parts in pieces)
    rows = sum(part.shape[0] for part in pieces[0])
    units, width = down.shape
    flat = [part for parts in pieces for part in parts]
    anywhere = pl.BlockSpec(memory_space=pl.ANY)
    return pl.pallas_call(
        functools.partial(expert_kernel, counts),
        out_shape=[jax.ShapeDtypeStruct((rows, width), jnp.bfloat16)] * steps,
        in_specs=[pl.BlockSpec(memory_space=pltpu.SMEM)] + [anywhere] * (len(flat) + 4),
        out_specs=[anywhere] * steps,
        scratch_shapes=[
            pltpu.VMEM((steps, rows, width), jnp.bfloat16),
            pltpu.VMEM((steps, 2, rows, units), jnp.bfloat16),
            pltpu.VMEM((width, units), jnp.bfloat16),
            pltpu.VMEM((width, units), jnp.bfloat16),
            pltpu.VMEM((units, width), jnp.bfloat16),
            pltpu.VMEM((rows, 2 * units), jnp.bfloat16),
            pltpu.VMEM((2, rows, width), jnp.bfloat16),
            pltpu.SemaphoreType.DMA((len(flat) + 1,)),
            pltpu.SemaphoreType.DMA((steps,)),
            pltpu.SemaphoreType.DMA((3,)),
            pltpu.SemaphoreType.DMA((steps,)),
        ],
        compiler_params=pltpu.CompilerParams(vmem_limit_bytes=48 * 1024 * 1024),
        cost_estimate=pl.CostEstimate(
            flops=6 * steps * rows * units * width,
            bytes_accessed=6 * units * width + steps * rows * (4 * width + 4 * units),
            transcendentals=steps * rows * units,
        ),
    )(blocks, *flat, saved, gate, up, down)


def expert_rounds(rows, saved, gate, up, down):
    me = lax.axis_index("seq")
    chips = lax.axis_size("seq") // 2
    z, core = me // 2, me % 2
    half = rows.shape[0] // 2

    def pair(by):
        there = 2 * ((z + by) % chips)
        return jnp.stack([there + core, there + 1 - core]).astype(jnp.int32)

    below = chip_shift(rows, 1)
    above = chip_shift(rows, -1)
    rows_other = core_swap(rows)
    here = expert_rows(pair(0), [[rows], [rows_other]], saved, gate, up, down)
    far_low = chip_shift(below[:half], 1)
    far_high = chip_shift(above[half:], -1)
    below_other = core_swap(below)
    above_other = core_swap(above)
    near = expert_rows(
        jnp.concatenate([pair(-1), pair(1)]),
        [[below], [below_other], [above], [above_other]],
        saved, gate, up, down,
    )
    far_low_other = core_swap(far_low)
    far_high_other = core_swap(far_high)
    far = expert_rows(
        pair(2), [[far_low, far_high], [far_low_other, far_high_other]], saved, gate, up, down
    )
    near_swapped = [core_swap(near[1]), core_swap(near[3])]
    here_swapped = core_swap(here[1])
    far_sum = added(far[0], core_swap(far[1])).astype(jnp.bfloat16)
    to_above = chip_shift(far_sum[:half], 1)
    to_below = chip_shift(far_sum[half:], -1)
    near_above = added(near[2], near_swapped[1])
    near_below = added(near[0], near_swapped[0])
    near_above = jnp.concatenate(
        [near_above[:half] + to_above.astype(jnp.float32), near_above[half:]]
    ).astype(jnp.bfloat16)
    near_below = jnp.concatenate(
        [near_below[:half], near_below[half:] + to_below.astype(jnp.float32)]
    ).astype(jnp.bfloat16)
    from_below = chip_shift(near_above, 1)
    from_above = chip_shift(near_below, -1)
    return added(here[0], here_swapped, from_below, from_above).astype(jnp.bfloat16)


def chained(block_states, log_sums, reach):
    blocks = log_sums.shape[0]
    me = lax.axis_index("seq")
    index = jnp.arange(blocks, dtype=jnp.int32)
    if reach == "before":
        taken = index < me
        crossed = (index[None, :] > index[:, None]) & (index[None, :] < me)
    else:
        taken = index > me
        crossed = (index[None, :] < index[:, None]) & (index[None, :] > me)
    exponent = jnp.sum(jnp.where(crossed[:, :, None], log_sums[None, :, :], 0.0), axis=1)
    share = jnp.where(taken[:, None], jnp.exp(exponent), 0.0)
    states = block_states.astype(jnp.float32).reshape(blocks, -1, log_sums.shape[1], HEAD)
    return jnp.sum(share[:, None, :, None] * states, axis=0)


def per_device(
    mixer_in,
    bc,
    log_decay,
    skip_gain,
    norm_gain,
    routes,
    route_weight,
    w_gate,
    w_up,
    w_down,
    saved_pre,
    d_out,
):
    row_count = mixer_in.shape[1]
    model_width = mixer_in.shape[2]
    head_count = log_decay.shape[2]
    head_size = model_width // head_count
    state_size = bc.shape[2] // 2
    expert_count = lax.axis_size("exp")
    capacity = saved_pre.shape[2] // (lax.axis_size("seq") * expert_count)
    per_token = routes.shape[2]
    values = mixer_in[0].astype(jnp.float32).reshape(row_count, head_count, head_size)
    write_raw = bc[0, :, :state_size]
    read_raw = bc[0, :, state_size:]
    write_rows = write_raw.astype(jnp.float32)
    read_rows = read_raw.astype(jnp.float32)
    log_rates = log_decay[0]
    cum_log = jnp.cumsum(log_rates, axis=0)
    flat_shape = (state_size, model_width)
    local_out, end_state = local_pass(
        span_forward, values, write_rows, read_rows, log_rates, write_raw, read_raw, False
    )
    log_sums = lax.all_gather(cum_log[-1], "seq")
    end_states = lax.all_gather(end_state.reshape(flat_shape).astype(jnp.bfloat16), "seq")
    incoming = chained(end_states, log_sums, "before")
    carried_in = jnp.einsum("tn,nhp->thp", read_rows, incoming, precision=HIGHEST)
    mixer_out = local_out + jnp.exp(cum_log)[:, :, None] * carried_in
    mixer_out = mixer_out + skip_gain[None, :, None] * values
    residual = (mixer_in[0].astype(jnp.float32) + mixer_out.reshape(row_count, model_width)).astype(
        jnp.bfloat16
    )
    chosen = routes[0].reshape(row_count * per_token)
    onehot = (chosen[:, None] == jnp.arange(expert_count, dtype=jnp.int32)[None, :]).astype(
        jnp.int32
    )
    before = jnp.cumsum(onehot, axis=0) - onehot
    slot_index = jnp.sum(before * onehot, axis=1)
    target = chosen * capacity + slot_index
    places = jnp.arange(expert_count * capacity, dtype=jnp.int32)
    picked = jnp.any(
        target.reshape(row_count, per_token)[:, :, None] == places[None, None, :], axis=1
    )
    packed = jnp.dot(
        picked.T.astype(jnp.bfloat16), d_out[0], preferred_element_type=jnp.float32
    ).astype(jnp.bfloat16)
    arrived = lax.all_to_all(
        packed.reshape(expert_count, capacity, model_width), "exp", 0, 0, tiled=True
    )
    summed = expert_rounds(
        arrived.reshape(expert_count * capacity, model_width),
        saved_pre, w_gate[0], w_up[0], w_down[0],
    )
    returned = lax.all_to_all(
        summed.reshape(expert_count, capacity, model_width), "exp", 0, 0, tiled=True
    )
    spread = jnp.sum(
        jnp.where(
            target.reshape(row_count, per_token)[:, :, None] == places[None, None, :],
            route_weight[0][:, :, None],
            0.0,
        ),
        axis=1,
    )
    moe_grad = jnp.dot(
        spread,
        returned.reshape(expert_count * capacity, model_width).astype(jnp.float32),
        precision=HIGHEST,
    )
    resid_float = residual.astype(jnp.float32)
    root_mean = jnp.sqrt(jnp.mean(resid_float * resid_float, axis=-1, keepdims=True) + EPSILON)
    normed = resid_float / root_mean
    scaled = moe_grad * norm_gain.astype(jnp.float32)[None, :]
    resid_grad = (
        d_out[0].astype(jnp.float32)
        + (scaled - normed * jnp.mean(scaled * normed, axis=-1, keepdims=True)) / root_mean
    )
    gradient = resid_grad.reshape(row_count, head_count, head_size)
    local_back, block_adjoint = local_pass(
        span_backward, gradient, write_rows, read_rows, log_rates, write_raw, read_raw, True
    )

    adjoints = lax.all_gather(block_adjoint.reshape(flat_shape).astype(jnp.bfloat16), "seq")
    after = chained(adjoints, log_sums, "after")
    to_end = jnp.exp(cum_log[-1][None, :] - cum_log)
    carried_back = jnp.einsum("sn,nhp->shp", write_rows, after, precision=HIGHEST)
    backward = local_back + to_end[:, :, None] * carried_back
    backward = backward + skip_gain[None, :, None] * gradient
    grad_in = (resid_grad + backward.reshape(row_count, model_width)).astype(jnp.bfloat16)
    return (residual[None], grad_in[None])


def solution(mesh):
    placed = (
        P("exp", "seq", None),
        P("exp", "seq", None),
        P("exp", "seq", None),
        P(),
        P(),
        P("exp", "seq", None),
        P("exp", "seq", None),
        P("exp", None, "seq"),
        P("exp", None, "seq"),
        P("exp", "seq", None),
        P("exp", None, None, "seq"),
        P("exp", "seq", None),
    )
    return jax.shard_map(
        per_device,
        mesh=mesh,
        in_specs=placed,
        out_specs=(P("exp", "seq", None), P("exp", "seq", None)),
        check_vma=False,
    )
```

```python
import functools

import jax
import jax.numpy as jnp
from jax import lax
from jax.experimental import pallas as pl
from jax.experimental.pallas import tpu as pltpu
from jax.sharding import PartitionSpec as P

HEAD = 64
PAIR = 2 * HEAD
STEP = 8
HIGHEST = lax.Precision.HIGHEST
EPSILON = 1e-05
MIB = 1024 * 1024
TILE = 1024
PARTS = 4
BY = (0, -1, 1, 2)


def chip_shift(value, by):
    chips = lax.axis_size("seq") // 2
    pairs = [(2 * z + c, 2 * ((z + by) % chips) + c) for z in range(chips) for c in range(2)]
    return lax.ppermute(value, "seq", pairs)


def core_swap(value):
    return lax.ppermute(value, "seq", [(i, i ^ 1) for i in range(lax.axis_size("seq"))])


def exact_dot(a, b, dims=((1,), (0,))):
    return lax.dot_general(
        a, b, (dims, ((), ())), precision=HIGHEST, preferred_element_type=jnp.float32
    )


def whole_call(body, outs, *args, flops=0, moved=0):
    vmem = pl.BlockSpec(memory_space=pltpu.VMEM)
    return pl.pallas_call(
        body,
        out_shape=[jax.ShapeDtypeStruct(shape, dtype) for shape, dtype in outs],
        in_specs=[vmem] * len(args),
        out_specs=[vmem] * len(outs),
        compiler_params=pltpu.CompilerParams(vmem_limit_bytes=32 * MIB),
        cost_estimate=pl.CostEstimate(flops=flops, bytes_accessed=moved, transcendentals=0),
    )(*args)


def added(*terms):
    total = terms[0].astype(jnp.float32)
    for term in terms[1:]:
        total = total + term.astype(jnp.float32)
    return total


def expert_kernel(places, *refs):
    count = steps = len(places)
    pieces, refs = refs[:count], refs[count:]
    saved, gate, up, down = refs[:4]
    outs, refs = refs[4 : 4 + count], refs[4 + count :]
    x, pre, w_gate, w_up, w_down, mixed, out, sem_x, sem_pre, sem_w, sem_out = refs
    part = pieces[0].shape[0]
    units, width = w_down.shape
    me = lax.axis_index("seq")
    chips = lax.axis_size("seq") // 2
    core = me % 2
    ahead = 1 - 2 * core

    def load(source, target, sem):
        rows = target.shape[0] // PARTS
        return [
            pltpu.make_async_copy(
                source.at[pl.ds(cut * rows, rows)], target.at[pl.ds(cut * rows, rows)], sem.at[cut]
            )
            for cut in range(PARTS)
        ]

    takes, befores, stores = [], [], []
    for piece, (away, along) in enumerate(places):
        chip = lax.rem(me // 2 + away + along * ahead + chips, chips)
        block = 2 * chip + (core if piece == 0 else 1 - core)
        start = pl.multiple_of(block * part, part)
        takes.append(load(pieces[piece], x.at[piece], sem_x.at[piece]))
        befores.append(
            [
                copy
                for kind in range(2)
                for copy in load(
                    saved.at[0, kind, pl.ds(start, part)], pre.at[piece, kind],
                    sem_pre.at[2 * piece + kind],
                )
            ]
        )
    cuts = [(low, min(low + 256, units)) for low in range(0, units, 256)]
    take_down = load(down, w_down, sem_w.at[0])
    take_rest = load(gate, w_gate, sem_w.at[1]) + load(up, w_up, sem_w.at[2])
    for copy in takes[0] + take_down + befores[0] + take_rest + takes[1] + befores[1]:
        copy.start()
    for step in range(steps):
        for copy in takes[step] + befores[step]:
            copy.wait()
        if step == 0:
            for copy in take_down:
                copy.wait()
        for low, high in cuts:
            hidden = lax.dot_general(
                x[step], w_down[low:high], (((1,), (1,)), ((), ())),
                preferred_element_type=jnp.float32,
            )
            gate_pre = pre[step, 0, :, low:high].astype(jnp.float32)
            up_pre = pre[step, 1, :, low:high].astype(jnp.float32)
            sigma = 0.5 * jnp.tanh(0.5 * gate_pre) + 0.5
            scaled = hidden * sigma
            mixed[step, :, low:high] = (scaled * up_pre * (1.0 + gate_pre * (1.0 - sigma))).astype(
                jnp.bfloat16
            )
            mixed[step, :, units + low : units + high] = (scaled * gate_pre).astype(jnp.bfloat16)
        if step == 0:
            for copy in take_rest:
                copy.wait()

        for low in range(0, width, TILE):
            weights = jnp.concatenate([w_gate[low : low + TILE], w_up[low : low + TILE]], axis=1)
            out[step, :, low : low + TILE] = lax.dot_general(
                mixed[step], weights, (((1,), (1,)), ((), ())),
                preferred_element_type=jnp.float32,
            ).astype(jnp.bfloat16)
            for half in range(2):
                store = pltpu.make_async_copy(
                    out.at[step, pl.ds(half * (part // 2), part // 2), pl.ds(low, TILE)],
                    outs[step].at[pl.ds(half * (part // 2), part // 2), pl.ds(low, TILE)],
                    sem_out.at[step, low // TILE, half],
                )
                store.start()
                stores.append(store)
    for store in stores:
        store.wait()


def expert_rows(places, pieces, saved, gate, up, down, cover=1.0):
    steps = count = len(pieces)
    rows = part = pieces[0].shape[0]
    units, width = down.shape
    anywhere = pl.BlockSpec(memory_space=pltpu.HBM)
    hbm = pl.BlockSpec(memory_space=pltpu.HBM)
    return pl.pallas_call(
        functools.partial(expert_kernel, places),
        out_shape=[jax.ShapeDtypeStruct((part, width), jnp.bfloat16)] * count,
        in_specs=[anywhere] * count + [hbm] * 4,
        out_specs=[anywhere] * count,
        scratch_shapes=[
            pltpu.VMEM((steps, rows, width), jnp.bfloat16),
            pltpu.VMEM((steps, 2, rows, units), jnp.bfloat16),
            pltpu.VMEM((width, units), jnp.bfloat16),
            pltpu.VMEM((width, units), jnp.bfloat16),
            pltpu.VMEM((units, width), jnp.bfloat16),
            pltpu.VMEM((steps, rows, 2 * units), jnp.bfloat16),
            pltpu.VMEM((steps, rows, width), jnp.bfloat16),
            pltpu.SemaphoreType.DMA((count, PARTS)),
            pltpu.SemaphoreType.DMA((2 * count, PARTS)),
            pltpu.SemaphoreType.DMA((3, PARTS)),
            pltpu.SemaphoreType.DMA((count, width // TILE, 2)),
        ],
        compiler_params=pltpu.CompilerParams(vmem_limit_bytes=60 * MIB),
        cost_estimate=pl.CostEstimate(
            flops=int(cover * 6 * count * part * units * width),
            bytes_accessed=int(cover * 6 * units * width),
            transcendentals=0,
        ),
    )(*pieces, saved, gate, up, down)


def mixer_local(x, bc, write_t, cum, cum_t, local, back_weights, state, grown, to_end):
    rows, width = x.shape
    heads = cum.shape[1]
    states = write_t.shape[0]
    write, read = bc[:, :states], bc[:, states:]
    dims = (((1,), (1,)), ((), ()))
    scores = lax.dot_general(read, write, dims, preferred_element_type=jnp.float32)
    scores_t = lax.dot_general(write, read, dims, preferred_element_type=jnp.float32)
    row = lax.broadcasted_iota(jnp.int32, (rows, rows), 0)
    col = lax.broadcasted_iota(jnp.int32, (rows, rows), 1)
    low_lanes = lax.broadcasted_iota(jnp.int32, (rows, PAIR), 1) < HEAD
    for pair in range(heads // 2):
        at = pair * PAIR
        values = x[:, at : at + PAIR].astype(jnp.float32)
        parts = []
        for head in (2 * pair, 2 * pair + 1):
            gap = cum[:, head : head + 1] - cum_t[head : head + 1, :]
            weights = jnp.where(row >= col, jnp.exp(jnp.minimum(gap, 0.0)), 0.0) * scores
            back_weights[head] = (
                jnp.where(col >= row, jnp.exp(jnp.minimum(-gap, 0.0)), 0.0) * scores_t
            )
            parts.append(exact_dot(weights, values))
        local[:, at : at + PAIR] = jnp.where(low_lanes, parts[0], parts[1])
    own = lax.broadcasted_iota(jnp.int32, (heads, width), 1) // HEAD
    spread = (own == lax.broadcasted_iota(jnp.int32, (heads, width), 0)).astype(jnp.float32)
    last = cum[rows - 1 : rows, :]
    grown[...] = exact_dot(jnp.exp(cum[...]), spread)
    ends = exact_dot(jnp.exp(last - cum[...]), spread)
    to_end[...] = ends
    added_state = exact_dot(write_t[...].astype(jnp.float32), ends * x[...].astype(jnp.float32))
    state[:states, :] = added_state.astype(jnp.bfloat16)
    sums = exact_dot(jnp.broadcast_to(last, (states, heads)), spread)
    term = lax.broadcasted_iota(jnp.int32, (states, width), 0)
    high = sums.astype(jnp.bfloat16).astype(jnp.float32)
    middle = (sums - high).astype(jnp.bfloat16).astype(jnp.float32)
    low = sums - high - middle
    terms = jnp.where(term == 0, high, jnp.where(term == 1, middle, jnp.where(term == 2, low, 0.0)))
    state[states:, :] = terms.astype(jnp.bfloat16)


def mixer_finish(x, local, bc, grown, skip, shares, states_own, states_other, residual, root):
    states = bc.shape[1] // 2
    blocks = states_own.shape[0]
    incoming = jnp.zeros((states, x.shape[1]), jnp.float32)
    for block in range(blocks):
        incoming += shares[block : block + 1, :] * states_own[block, :states].astype(jnp.float32)
        incoming += shares[blocks + block : blocks + block + 1, :] * states_other[block, :states].astype(jnp.float32)
    carried = exact_dot(bc[:, states:].astype(jnp.float32), incoming)
    values = x[...].astype(jnp.float32)
    total = values + (local[...] + grown[...] * carried + skip[...] * values)
    rounded = total.astype(jnp.bfloat16)
    residual[...] = rounded
    again = rounded.astype(jnp.float32)
    root[...] = jnp.sqrt(jnp.mean(again * again, axis=-1, keepdims=True) + EPSILON)


def weighed(weights, rows):
    count = weights.shape[0]
    high = weights.astype(jnp.bfloat16)
    rest = (weights - high.astype(jnp.float32)).astype(jnp.bfloat16)
    both = lax.dot_general(
        jnp.concatenate([high, rest], axis=0), rows, (((1,), (0,)), ((), ())),
        preferred_element_type=jnp.float32,
    )
    return both[:count] + both[count:]


def weighed_rows(returned, spread, out):
    out[...] = weighed(spread[...], returned[...]).astype(jnp.bfloat16)


def padded_sum(room, capacity, *refs):
    terms, out = refs[:-1], refs[-1]
    total = terms[0][...].astype(jnp.float32)
    for term in terms[1:]:
        total = total + term[...].astype(jnp.float32)
    place = lax.broadcasted_iota(jnp.int32, (out.shape[0], total.shape[0]), 0)
    row = lax.broadcasted_iota(jnp.int32, (out.shape[0], total.shape[0]), 1)
    slot = place % room
    opened = ((slot < capacity) & (row == (place // room) * capacity + slot)).astype(jnp.float32)
    out[...] = lax.dot_general(
        opened.astype(jnp.bfloat16), total.astype(jnp.bfloat16), (((1,), (0,)), ((), ())),
        preferred_element_type=jnp.float32,
    ).astype(jnp.bfloat16)


def padded(room, capacity, *terms):
    rows, width = terms[0].shape
    count = rows // capacity * room
    tile = 512
    return pl.pallas_call(
        functools.partial(padded_sum, room, capacity),
        out_shape=jax.ShapeDtypeStruct((count, width), jnp.bfloat16),
        grid=(width // tile,),
        in_specs=[pl.BlockSpec((rows, tile), lambda i: (0, i))] * len(terms),
        out_specs=pl.BlockSpec((count, tile), lambda i: (0, i)),
        compiler_params=pltpu.CompilerParams(vmem_limit_bytes=24 * MIB),
        cost_estimate=pl.CostEstimate(
            flops=2 * rows * count * width, bytes_accessed=2 * (len(terms) + 1) * rows * width,
            transcendentals=0,
        ),
    )(*terms)


def norm_back(returned, spread, passed, residual, root, gain, d_out, read_t, grown, resid_grad, adjoint):
    moe_grad = weighed(spread[...], returned[...]) + passed[...].astype(jnp.float32)
    scaled = moe_grad * gain[...]
    normed = residual[...].astype(jnp.float32) / root[...]
    along = jnp.mean(scaled * normed, axis=-1, keepdims=True)
    gradient = d_out[...].astype(jnp.float32) + (scaled - normed * along) / root[...]
    resid_grad[...] = gradient
    adjoint[...] = exact_dot(read_t[...].astype(jnp.float32), grown[...] * gradient).astype(
        jnp.bfloat16
    )


def back_local(resid_grad, back_weights, skip, base):
    rows = resid_grad.shape[0]
    low_lanes = lax.broadcasted_iota(jnp.int32, (rows, PAIR), 1) < HEAD
    for pair in range(back_weights.shape[0] // 2):
        at = pair * PAIR
        gradient = resid_grad[:, at : at + PAIR]
        first = exact_dot(back_weights[2 * pair], gradient)
        second = exact_dot(back_weights[2 * pair + 1], gradient)
        mixed = jnp.where(low_lanes, first, second)
        base[:, at : at + PAIR] = gradient + (mixed + skip[:, at : at + PAIR] * gradient)


def back_finish(base, bc, to_end, shares, own, other, grad_in):
    states = bc.shape[1] // 2
    blocks = own.shape[0]
    after = jnp.zeros((states, base.shape[1]), jnp.float32)
    for block in range(blocks):
        after += shares[block : block + 1, :] * own[block].astype(jnp.float32)
        after += shares[blocks + block : blocks + block + 1, :] * other[block].astype(jnp.float32)
    carried = exact_dot(bc[:, :states].astype(jnp.float32), after)
    grad_in[...] = (base[...] + to_end[...] * carried).astype(jnp.bfloat16)


def block_ids():
    me = lax.axis_index("seq")
    chips = lax.axis_size("seq") // 2
    z, core = me // 2, me % 2
    there = [2 * ((z + by) % chips) for by in BY]
    return jnp.stack([t + core for t in there] + [t + 1 - core for t in there]).astype(jnp.int32)


def all_blocks(value, *earlier):
    own = jnp.stack([value] + [chip_shift(value, -by) for by in BY[1:]])
    own = after(own, *earlier)
    return own, core_swap(own)


def shares_of(ids, log_sums, backwards):
    me = lax.axis_index("seq")
    place = -ids if backwards else ids
    here = -me if backwards else me
    crossed = (place[None, :] > place[:, None]) & (place[None, :] < here)
    exponent = jnp.sum(jnp.where(crossed[:, :, None], log_sums[None], 0.0), axis=1)
    return jnp.where((place < here)[:, None], jnp.exp(exponent), 0.0)


def tied(*values):
    return lax.optimization_barrier(values)


def after(value, *others):
    return lax.optimization_barrier((value, *others))[0]


def along_shift(value, by):
    chips = lax.axis_size("seq") // 2
    pairs = [
        (2 * z + c, 2 * ((z + by * (1 - 2 * c)) % chips) + c) for z in range(chips) for c in range(2)
    ]
    return lax.ppermute(value, "seq", pairs)


def close_up(room, capacity, arrived, out):
    parts = 2
    count, rows = out.shape[0] // parts, arrived.shape[0] // parts
    place = lax.broadcasted_iota(jnp.int32, (count, rows), 0)
    row = lax.broadcasted_iota(jnp.int32, (count, rows), 1)
    kept = row == (place // capacity) * room + place % capacity
    kept = kept.astype(jnp.float32).astype(jnp.bfloat16)
    for part in range(parts):
        out[part * count : (part + 1) * count] = lax.dot_general(
            kept, arrived[part * rows : (part + 1) * rows], (((1,), (0,)), ((), ())),
            preferred_element_type=jnp.float32,
        ).astype(jnp.bfloat16)


def closed_up(arrived, capacity):
    experts, room, width = arrived.shape
    tile = 512
    count = experts * capacity
    return pl.pallas_call(
        functools.partial(close_up, room, capacity),
        out_shape=jax.ShapeDtypeStruct((count, width), jnp.bfloat16),
        grid=(width // tile,),
        in_specs=[pl.BlockSpec((experts * room, tile), lambda i: (0, i))],
        out_specs=pl.BlockSpec((count, tile), lambda i: (0, i)),
        compiler_params=pltpu.CompilerParams(vmem_limit_bytes=24 * MIB),
        cost_estimate=pl.CostEstimate(
            flops=experts * room * count * width, bytes_accessed=4 * count * width,
            transcendentals=0,
        ),
    )(arrived.reshape(experts * room, width))


def per_device(
    mixer_in,
    bc,
    log_decay,
    skip_gain,
    norm_gain,
    routes,
    route_weight,
    w_gate,
    w_up,
    w_down,
    saved_pre,
    d_out,
):
    row_count = mixer_in.shape[1]
    width = mixer_in.shape[2]
    heads = log_decay.shape[2]
    states = bc.shape[2] // 2
    expert_count = lax.axis_size("exp")
    capacity = saved_pre.shape[2] // (lax.axis_size("seq") * expert_count)
    room = -(-capacity // STEP) * STEP
    per_token = routes.shape[2]
    whole, table = ((row_count, width), jnp.float32), ((heads, row_count, row_count), jnp.float32)
    ids = block_ids()

    chosen = routes[0].reshape(row_count * per_token)
    onehot = (chosen[:, None] == jnp.arange(expert_count, dtype=jnp.int32)[None, :]).astype(
        jnp.int32
    )
    earlier = jnp.cumsum(onehot, axis=0) - onehot
    slot_index = jnp.sum(earlier * onehot, axis=1)
    target = (chosen * room + slot_index).reshape(row_count, per_token)
    places = jnp.arange(expert_count * room, dtype=jnp.int32)
    notes = jnp.concatenate([target.astype(jnp.float32), route_weight[0]], axis=1)

    def slotted(target, weight, rows):
        hit = target[:, :, None] == places[None, None, :]
        spread = jnp.sum(jnp.where(hit, weight[:, :, None], 0.0), axis=1)
        picked = jnp.any(hit, axis=1).T.astype(jnp.bfloat16)
        packed = jnp.dot(picked, rows, preferred_element_type=jnp.float32).astype(jnp.bfloat16)
        return spread, packed.reshape(expert_count, room, width)

    spread, packed = slotted(target, route_weight[0], d_out[0])
    d_out_passed = along_shift(after(d_out[0], packed), -1)
    notes_passed = along_shift(notes, -1)
    spread_passed, packed_passed = slotted(
        notes_passed[:, :per_token].astype(jnp.int32), notes_passed[:, per_token:], d_out_passed
    )

    arrived = lax.all_to_all(packed, "exp", 0, 0, tiled=True)
    log_rates = after(log_decay[0], packed)

    cum = jnp.cumsum(log_rates, axis=0)
    skip = jnp.repeat(skip_gain, HEAD)[None, :]
    local, back_weights, state, grown, to_end = whole_call(
        mixer_local,
        [whole, table, ((2 * states, width), jnp.bfloat16), whole, whole],
        mixer_in[0], bc[0], bc[0, :, :states].T, cum, cum.T,
        flops=2 * 6 * 2 * row_count * row_count * width, moved=8 * MIB,
    )
    states_own, states_other = all_blocks(state, d_out_passed)
    log_sums = jnp.concatenate([states_own[:, states:], states_other[:, states:]])
    log_sums = jnp.sum(log_sums.astype(jnp.float32), axis=1)
    arrived, states_own, states_other, log_sums = tied(arrived, states_own, states_other, log_sums)
    arrived = after(arrived, d_out_passed, notes_passed)
    packed_passed = after(packed_passed, arrived)
    shares = shares_of(ids, log_sums, False)
    shares_back = shares_of(ids, log_sums, True)
    weights = (saved_pre, w_gate[0], w_up[0], w_down[0])
    rows = closed_up(arrived, capacity)
    ring = along_shift(rows, 1)
    arrived_passed = lax.all_to_all(packed_passed, "exp", 0, 0, tiled=True)
    here, here_rest = expert_rows(((0, 0), (0, 0)), [rows, core_swap(rows)], *weights)
    ring = after(ring, here)
    far = along_shift(ring, 1)
    ring, ring_rest = expert_rows(
        ((0, -1), (0, 1)), [ring, core_swap(ring)], *weights, cover=0.05
    )
    arrived_passed = after(arrived_passed, ring, far)
    passed = closed_up(arrived_passed, capacity)
    passed, passed_rest = expert_rows(
        ((0, 1), (0, -1)), [passed, core_swap(passed)], *weights
    )
    far = after(far, passed)
    far, far_rest = expert_rows(((2, 0), (2, 0)), [far, core_swap(far)], *weights)
    far_sum = added(far, core_swap(far_rest)).astype(jnp.bfloat16)
    far_back = along_shift(far_sum, -1)
    sent_passed = padded(room, capacity, passed, core_swap(passed_rest))
    returned_passed = lax.all_to_all(
        sent_passed.reshape(expert_count, room, width), "exp", 0, 0, tiled=True
    )
    ring_sum = added(ring, core_swap(ring_rest), after(far_back, sent_passed)).astype(jnp.bfloat16)
    ring_back = along_shift(ring_sum, -1)
    sent = padded(room, capacity, here, core_swap(here_rest), ring_back)
    sent, returned_passed = tied(sent, returned_passed)
    returned = lax.all_to_all(
        sent.reshape(expert_count, room, width), "exp", 0, 0, tiled=True
    )
    (moe_passed,) = whole_call(
        weighed_rows, [((row_count, width), jnp.bfloat16)],
        returned_passed.reshape(expert_count * room, width), spread_passed,
        flops=4 * expert_count * room * row_count * width, moved=3 * MIB,
    )
    moe_passed = along_shift(moe_passed, 1)
    residual, root = whole_call(
        mixer_finish,
        [((row_count, width), jnp.bfloat16), ((row_count, 1), jnp.float32)],
        mixer_in[0], local, bc[0], grown, skip, shares, states_own, states_other,
        flops=2 * 6 * states * row_count * width, moved=6 * MIB,
    )
    resid_grad, adjoint = whole_call(
        norm_back,
        [whole, ((states, width), jnp.bfloat16)],
        returned.reshape(expert_count * room, width), spread, moe_passed, residual, root,
        norm_gain.astype(jnp.float32)[None, :], d_out[0], bc[0, :, states:].T, grown,
        flops=4 * expert_count * room * row_count * width, moved=6 * MIB,
    )
    (base,) = whole_call(
        back_local, [whole], resid_grad, back_weights, skip,
        flops=2 * 6 * 2 * row_count * row_count * width, moved=4 * MIB,
    )
    adjoints_own, adjoints_other = all_blocks(adjoint)
    (grad_in,) = whole_call(
        back_finish, [((row_count, width), jnp.bfloat16)],
        base, bc[0], to_end, shares_back, adjoints_own, adjoints_other,
        flops=2 * 6 * states * row_count * width, moved=4 * MIB,
    )
    return (residual[None], grad_in[None])


def solution(mesh):
    placed = (
        P("exp", "seq", None),
        P("exp", "seq", None),
        P("exp", "seq", None),
        P(),
        P(),
        P("exp", "seq", None),
        P("exp", "seq", None),
        P("exp", None, "seq"),
        P("exp", None, "seq"),
        P("exp", "seq", None),
        P("exp", None, None, "seq"),
        P("exp", "seq", None),
    )
    return jax.shard_map(
        per_device,
        mesh=mesh,
        in_specs=placed,
        out_specs=(P("exp", "seq", None), P("exp", "seq", None)),
        check_vma=False,
    )
```

```python
import functools

import jax
import jax.numpy as jnp
from jax import lax
from jax.experimental import pallas as pl
from jax.experimental.pallas import tpu as pltpu
from jax.sharding import PartitionSpec as P

HEAD = 64
PAIR = 2 * HEAD
STEP = 8
HIGHEST = lax.Precision.HIGHEST
EPSILON = 1e-05
MIB = 1024 * 1024
TILE = 1024
PARTS = 4
BY = (0, -1, 1, 2)


def chip_shift(value, by):
    chips = lax.axis_size("seq") // 2
    pairs = [(2 * z + c, 2 * ((z + by) % chips) + c) for z in range(chips) for c in range(2)]
    return lax.ppermute(value, "seq", pairs)


def core_swap(value):
    return lax.ppermute(value, "seq", [(i, i ^ 1) for i in range(lax.axis_size("seq"))])


def exact_dot(a, b, dims=((1,), (0,))):
    return lax.dot_general(
        a, b, (dims, ((), ())), precision=HIGHEST, preferred_element_type=jnp.float32
    )


def whole_call(body, outs, *args, flops=0, moved=0):
    vmem = pl.BlockSpec(memory_space=pltpu.VMEM)
    return pl.pallas_call(
        body,
        out_shape=[jax.ShapeDtypeStruct(shape, dtype) for shape, dtype in outs],
        in_specs=[vmem] * len(args),
        out_specs=[vmem] * len(outs),
        compiler_params=pltpu.CompilerParams(vmem_limit_bytes=32 * MIB),
        cost_estimate=pl.CostEstimate(flops=flops, bytes_accessed=moved, transcendentals=0),
    )(*args)


def added(*terms):
    total = terms[0].astype(jnp.float32)
    for term in terms[1:]:
        total = total + term.astype(jnp.float32)
    return total


def expert_kernel(places, *refs):
    count = steps = len(places)
    pieces, refs = refs[:count], refs[count:]
    saved, gate, up, down = refs[:4]
    outs, refs = refs[4 : 4 + count], refs[4 + count :]
    x, pre, w_gate, w_up, w_down, mixed, out, sem_x, sem_pre, sem_w, sem_out = refs
    part = pieces[0].shape[0]
    units, width = w_down.shape
    me = lax.axis_index("seq")
    chips = lax.axis_size("seq") // 2
    core = me % 2
    ahead = 1 - 2 * core

    def load(source, target, sem):
        rows = target.shape[0] // PARTS
        return [
            pltpu.make_async_copy(
                source.at[pl.ds(cut * rows, rows)], target.at[pl.ds(cut * rows, rows)], sem.at[cut]
            )
            for cut in range(PARTS)
        ]

    takes, befores, stores = [], [], []
    for piece, (away, along) in enumerate(places):
        chip = lax.rem(me // 2 + away + along * ahead + chips, chips)
        block = 2 * chip + (core if piece == 0 else 1 - core)
        start = pl.multiple_of(block * part, part)
        takes.append(load(pieces[piece], x.at[piece], sem_x.at[piece]))
        befores.append(
            [
                copy
                for kind in range(2)
                for copy in load(
                    saved.at[0, kind, pl.ds(start, part)], pre.at[piece, kind],
                    sem_pre.at[2 * piece + kind],
                )
            ]
        )
    cuts = [(low, min(low + 256, units)) for low in range(0, units, 256)]
    take_down = load(down, w_down, sem_w.at[0])
    take_rest = load(gate, w_gate, sem_w.at[1]) + load(up, w_up, sem_w.at[2])
    for copy in takes[0] + take_down + befores[0] + take_rest + takes[1] + befores[1]:
        copy.start()
    for step in range(steps):
        for copy in takes[step] + befores[step]:
            copy.wait()
        if step == 0:
            for copy in take_down:
                copy.wait()
        for low, high in cuts:
            hidden = lax.dot_general(
                x[step], w_down[low:high], (((1,), (1,)), ((), ())),
                preferred_element_type=jnp.float32,
            )
            gate_pre = pre[step, 0, :, low:high].astype(jnp.float32)
            up_pre = pre[step, 1, :, low:high].astype(jnp.float32)
            sigma = 0.5 * jnp.tanh(0.5 * gate_pre) + 0.5
            scaled = hidden * sigma
            mixed[step, :, low:high] = (scaled * up_pre * (1.0 + gate_pre * (1.0 - sigma))).astype(
                jnp.bfloat16
            )
            mixed[step, :, units + low : units + high] = (scaled * gate_pre).astype(jnp.bfloat16)
        if step == 0:
            for copy in take_rest:
                copy.wait()

        for low in range(0, width, TILE):
            weights = jnp.concatenate([w_gate[low : low + TILE], w_up[low : low + TILE]], axis=1)
            out[step, :, low : low + TILE] = lax.dot_general(
                mixed[step], weights, (((1,), (1,)), ((), ())),
                preferred_element_type=jnp.float32,
            ).astype(jnp.bfloat16)
            for half in range(2):
                store = pltpu.make_async_copy(
                    out.at[step, pl.ds(half * (part // 2), part // 2), pl.ds(low, TILE)],
                    outs[step].at[pl.ds(half * (part // 2), part // 2), pl.ds(low, TILE)],
                    sem_out.at[step, low // TILE, half],
                )
                store.start()
                stores.append(store)
    for store in stores:
        store.wait()


def expert_rows(places, pieces, saved, gate, up, down, cover=1.0):
    steps = count = len(pieces)
    rows = part = pieces[0].shape[0]
    units, width = down.shape
    anywhere = pl.BlockSpec(memory_space=pltpu.HBM)
    hbm = pl.BlockSpec(memory_space=pltpu.HBM)
    return pl.pallas_call(
        functools.partial(expert_kernel, places),
        out_shape=[jax.ShapeDtypeStruct((part, width), jnp.bfloat16)] * count,
        in_specs=[anywhere] * count + [hbm] * 4,
        out_specs=[anywhere] * count,
        scratch_shapes=[
            pltpu.VMEM((steps, rows, width), jnp.bfloat16),
            pltpu.VMEM((steps, 2, rows, units), jnp.bfloat16),
            pltpu.VMEM((width, units), jnp.bfloat16),
            pltpu.VMEM((width, units), jnp.bfloat16),
            pltpu.VMEM((units, width), jnp.bfloat16),
            pltpu.VMEM((steps, rows, 2 * units), jnp.bfloat16),
            pltpu.VMEM((steps, rows, width), jnp.bfloat16),
            pltpu.SemaphoreType.DMA((count, PARTS)),
            pltpu.SemaphoreType.DMA((2 * count, PARTS)),
            pltpu.SemaphoreType.DMA((3, PARTS)),
            pltpu.SemaphoreType.DMA((count, width // TILE, 2)),
        ],
        compiler_params=pltpu.CompilerParams(vmem_limit_bytes=60 * MIB),
        cost_estimate=pl.CostEstimate(
            flops=int(cover * 6 * count * part * units * width),
            bytes_accessed=int(cover * 6 * units * width),
            transcendentals=0,
        ),
    )(*pieces, saved, gate, up, down)


def mixer_local(x, bc, write_t, cum, cum_t, local, back_weights, state, grown, to_end):
    rows, width = x.shape
    heads = cum.shape[1]
    states = write_t.shape[0]
    write, read = bc[:, :states], bc[:, states:]
    dims = (((1,), (1,)), ((), ()))
    scores = lax.dot_general(read, write, dims, preferred_element_type=jnp.float32)
    scores_t = lax.dot_general(write, read, dims, preferred_element_type=jnp.float32)
    row = lax.broadcasted_iota(jnp.int32, (rows, rows), 0)
    col = lax.broadcasted_iota(jnp.int32, (rows, rows), 1)
    low_lanes = lax.broadcasted_iota(jnp.int32, (rows, PAIR), 1) < HEAD
    for pair in range(heads // 2):
        at = pair * PAIR
        values = x[:, at : at + PAIR].astype(jnp.float32)
        parts = []
        for head in (2 * pair, 2 * pair + 1):
            gap = cum[:, head : head + 1] - cum_t[head : head + 1, :]
            weights = jnp.where(row >= col, jnp.exp(jnp.minimum(gap, 0.0)), 0.0) * scores
            back_weights[head] = (
                jnp.where(col >= row, jnp.exp(jnp.minimum(-gap, 0.0)), 0.0) * scores_t
            )
            parts.append(exact_dot(weights, values))
        local[:, at : at + PAIR] = jnp.where(low_lanes, parts[0], parts[1])
    own = lax.broadcasted_iota(jnp.int32, (heads, width), 1) // HEAD
    spread = (own == lax.broadcasted_iota(jnp.int32, (heads, width), 0)).astype(jnp.float32)
    last = cum[rows - 1 : rows, :]
    grown[...] = exact_dot(jnp.exp(cum[...]), spread)
    ends = exact_dot(jnp.exp(last - cum[...]), spread)
    to_end[...] = ends
    added_state = exact_dot(write_t[...].astype(jnp.float32), ends * x[...].astype(jnp.float32))
    state[:states, :] = added_state.astype(jnp.bfloat16)
    sums = exact_dot(jnp.broadcast_to(last, (states, heads)), spread)
    term = lax.broadcasted_iota(jnp.int32, (states, width), 0)
    high = sums.astype(jnp.bfloat16).astype(jnp.float32)
    middle = (sums - high).astype(jnp.bfloat16).astype(jnp.float32)
    low = sums - high - middle
    terms = jnp.where(term == 0, high, jnp.where(term == 1, middle, jnp.where(term == 2, low, 0.0)))
    state[states:, :] = terms.astype(jnp.bfloat16)


def mixer_finish(x, local, bc, grown, skip, shares, states_own, states_other, residual, root):
    states = bc.shape[1] // 2
    blocks = states_own.shape[0]
    incoming = jnp.zeros((states, x.shape[1]), jnp.float32)
    for block in range(blocks):
        incoming += shares[block : block + 1, :] * states_own[block, :states].astype(jnp.float32)
        incoming += shares[blocks + block : blocks + block + 1, :] * states_other[block, :states].astype(jnp.float32)
    carried = exact_dot(bc[:, states:].astype(jnp.float32), incoming)
    values = x[...].astype(jnp.float32)
    total = values + (local[...] + grown[...] * carried + skip[...] * values)
    rounded = total.astype(jnp.bfloat16)
    residual[...] = rounded
    again = rounded.astype(jnp.float32)
    root[...] = jnp.sqrt(jnp.mean(again * again, axis=-1, keepdims=True) + EPSILON)


def weighed(weights, rows):
    count = weights.shape[0]
    high = weights.astype(jnp.bfloat16)
    rest = (weights - high.astype(jnp.float32)).astype(jnp.bfloat16)
    both = lax.dot_general(
        jnp.concatenate([high, rest], axis=0), rows, (((1,), (0,)), ((), ())),
        preferred_element_type=jnp.float32,
    )
    return both[:count] + both[count:]


def weighed_rows(returned, spread, out):
    out[...] = weighed(spread[...], returned[...]).astype(jnp.bfloat16)


def padded_sum(room, capacity, *refs):
    terms, out = refs[:-1], refs[-1]
    total = terms[0][...].astype(jnp.float32)
    for term in terms[1:]:
        total = total + term[...].astype(jnp.float32)
    place = lax.broadcasted_iota(jnp.int32, (out.shape[0], total.shape[0]), 0)
    row = lax.broadcasted_iota(jnp.int32, (out.shape[0], total.shape[0]), 1)
    slot = place % room
    opened = ((slot < capacity) & (row == (place // room) * capacity + slot)).astype(jnp.float32)
    out[...] = lax.dot_general(
        opened.astype(jnp.bfloat16), total.astype(jnp.bfloat16), (((1,), (0,)), ((), ())),
        preferred_element_type=jnp.float32,
    ).astype(jnp.bfloat16)


def padded(room, capacity, *terms):
    rows, width = terms[0].shape
    count = rows // capacity * room
    tile = 512
    return pl.pallas_call(
        functools.partial(padded_sum, room, capacity),
        out_shape=jax.ShapeDtypeStruct((count, width), jnp.bfloat16),
        grid=(width // tile,),
        in_specs=[pl.BlockSpec((rows, tile), lambda i: (0, i))] * len(terms),
        out_specs=pl.BlockSpec((count, tile), lambda i: (0, i)),
        compiler_params=pltpu.CompilerParams(vmem_limit_bytes=24 * MIB),
        cost_estimate=pl.CostEstimate(
            flops=2 * rows * count * width, bytes_accessed=2 * (len(terms) + 1) * rows * width,
            transcendentals=0,
        ),
    )(*terms)


def norm_back(returned, spread, passed, residual, root, gain, d_out, read_t, grown, resid_grad, adjoint):
    moe_grad = weighed(spread[...], returned[...]) + passed[...].astype(jnp.float32)
    scaled = moe_grad * gain[...]
    normed = residual[...].astype(jnp.float32) / root[...]
    along = jnp.mean(scaled * normed, axis=-1, keepdims=True)
    gradient = d_out[...].astype(jnp.float32) + (scaled - normed * along) / root[...]
    resid_grad[...] = gradient
    adjoint[...] = exact_dot(read_t[...].astype(jnp.float32), grown[...] * gradient).astype(
        jnp.bfloat16
    )


def back_local(resid_grad, back_weights, skip, base):
    rows = resid_grad.shape[0]
    low_lanes = lax.broadcasted_iota(jnp.int32, (rows, PAIR), 1) < HEAD
    for pair in range(back_weights.shape[0] // 2):
        at = pair * PAIR
        gradient = resid_grad[:, at : at + PAIR]
        first = exact_dot(back_weights[2 * pair], gradient)
        second = exact_dot(back_weights[2 * pair + 1], gradient)
        mixed = jnp.where(low_lanes, first, second)
        base[:, at : at + PAIR] = gradient + (mixed + skip[:, at : at + PAIR] * gradient)


def back_finish(base, bc, to_end, shares, own, other, grad_in):
    states = bc.shape[1] // 2
    blocks = own.shape[0]
    after = jnp.zeros((states, base.shape[1]), jnp.float32)
    for block in range(blocks):
        after += shares[block : block + 1, :] * own[block].astype(jnp.float32)
        after += shares[blocks + block : blocks + block + 1, :] * other[block].astype(jnp.float32)
    carried = exact_dot(bc[:, :states].astype(jnp.float32), after)
    grad_in[...] = (base[...] + to_end[...] * carried).astype(jnp.bfloat16)


def block_ids():
    me = lax.axis_index("seq")
    chips = lax.axis_size("seq") // 2
    z, core = me // 2, me % 2
    there = [2 * ((z + by) % chips) for by in BY]
    return jnp.stack([t + core for t in there] + [t + 1 - core for t in there]).astype(jnp.int32)


def all_blocks(value, *earlier):
    own = jnp.stack([value] + [chip_shift(value, -by) for by in BY[1:]])
    own = after(own, *earlier)
    return own, core_swap(own)


def shares_of(ids, log_sums, backwards):
    me = lax.axis_index("seq")
    place = -ids if backwards else ids
    here = -me if backwards else me
    crossed = (place[None, :] > place[:, None]) & (place[None, :] < here)
    exponent = jnp.sum(jnp.where(crossed[:, :, None], log_sums[None], 0.0), axis=1)
    return jnp.where((place < here)[:, None], jnp.exp(exponent), 0.0)


def tied(*values):
    return lax.optimization_barrier(values)


def after(value, *others):
    return lax.optimization_barrier((value, *others))[0]


def along_shift(value, by):
    chips = lax.axis_size("seq") // 2
    pairs = [
        (2 * z + c, 2 * ((z + by * (1 - 2 * c)) % chips) + c) for z in range(chips) for c in range(2)
    ]
    return lax.ppermute(value, "seq", pairs)


def close_up(room, capacity, arrived, out):
    parts = 2
    count, rows = out.shape[0] // parts, arrived.shape[0] // parts
    place = lax.broadcasted_iota(jnp.int32, (count, rows), 0)
    row = lax.broadcasted_iota(jnp.int32, (count, rows), 1)
    kept = row == (place // capacity) * room + place % capacity
    kept = kept.astype(jnp.float32).astype(jnp.bfloat16)
    for part in range(parts):
        out[part * count : (part + 1) * count] = lax.dot_general(
            kept, arrived[part * rows : (part + 1) * rows], (((1,), (0,)), ((), ())),
            preferred_element_type=jnp.float32,
        ).astype(jnp.bfloat16)


def closed_up(arrived, capacity):
    experts, room, width = arrived.shape
    tile = 512
    count = experts * capacity
    return pl.pallas_call(
        functools.partial(close_up, room, capacity),
        out_shape=jax.ShapeDtypeStruct((count, width), jnp.bfloat16),
        grid=(width // tile,),
        in_specs=[pl.BlockSpec((experts * room, tile), lambda i: (0, i))],
        out_specs=pl.BlockSpec((count, tile), lambda i: (0, i)),
        compiler_params=pltpu.CompilerParams(vmem_limit_bytes=24 * MIB),
        cost_estimate=pl.CostEstimate(
            flops=experts * room * count * width, bytes_accessed=4 * count * width,
            transcendentals=0,
        ),
    )(arrived.reshape(experts * room, width))


def per_device(
    mixer_in,
    bc,
    log_decay,
    skip_gain,
    norm_gain,
    routes,
    route_weight,
    w_gate,
    w_up,
    w_down,
    saved_pre,
    d_out,
):
    row_count = mixer_in.shape[1]
    width = mixer_in.shape[2]
    heads = log_decay.shape[2]
    states = bc.shape[2] // 2
    expert_count = lax.axis_size("exp")
    capacity = saved_pre.shape[2] // (lax.axis_size("seq") * expert_count)
    room = -(-capacity // STEP) * STEP
    per_token = routes.shape[2]
    whole, table = ((row_count, width), jnp.float32), ((heads, row_count, row_count), jnp.float32)
    ids = block_ids()

    chosen = routes[0].reshape(row_count * per_token)
    onehot = (chosen[:, None] == jnp.arange(expert_count, dtype=jnp.int32)[None, :]).astype(
        jnp.int32
    )
    earlier = jnp.cumsum(onehot, axis=0) - onehot
    slot_index = jnp.sum(earlier * onehot, axis=1)
    target = (chosen * room + slot_index).reshape(row_count, per_token)
    places = jnp.arange(expert_count * room, dtype=jnp.int32)
    notes = jnp.concatenate([target.astype(jnp.float32), route_weight[0]], axis=1)

    def slotted(target, weight, rows):
        hit = target[:, :, None] == places[None, None, :]
        spread = jnp.sum(jnp.where(hit, weight[:, :, None], 0.0), axis=1)
        picked = jnp.any(hit, axis=1).T.astype(jnp.bfloat16)
        packed = jnp.dot(picked, rows, preferred_element_type=jnp.float32).astype(jnp.bfloat16)
        return spread, packed.reshape(expert_count, room, width)

    spread, packed = slotted(target, route_weight[0], d_out[0])
    d_out_passed = along_shift(after(d_out[0], packed), -1)
    notes_passed = along_shift(notes, -1)
    spread_passed, packed_passed = slotted(
        notes_passed[:, :per_token].astype(jnp.int32), notes_passed[:, per_token:], d_out_passed
    )

    arrived = lax.all_to_all(packed, "exp", 0, 0, tiled=True)
    log_rates = after(log_decay[0], packed)

    cum = jnp.cumsum(log_rates, axis=0)
    skip = jnp.repeat(skip_gain, HEAD)[None, :]
    local, back_weights, state, grown, to_end = whole_call(
        mixer_local,
        [whole, table, ((2 * states, width), jnp.bfloat16), whole, whole],
        mixer_in[0], bc[0], bc[0, :, :states].T, cum, cum.T,
        flops=2 * 6 * 2 * row_count * row_count * width, moved=8 * MIB,
    )
    states_own, states_other = all_blocks(state, d_out_passed)
    log_sums = jnp.concatenate([states_own[:, states:], states_other[:, states:]])
    log_sums = jnp.sum(log_sums.astype(jnp.float32), axis=1)
    arrived, states_own, states_other, log_sums = tied(arrived, states_own, states_other, log_sums)
    arrived = after(arrived, d_out_passed, notes_passed)
    packed_passed = after(packed_passed, arrived)
    shares = shares_of(ids, log_sums, False)
    shares_back = shares_of(ids, log_sums, True)
    weights = (saved_pre, w_gate[0], w_up[0], w_down[0])
    rows = closed_up(arrived, capacity)
    ring = along_shift(rows, 1)
    arrived_passed = lax.all_to_all(packed_passed, "exp", 0, 0, tiled=True)
    here, here_rest = expert_rows(((0, 0), (0, 0)), [rows, core_swap(rows)], *weights)
    ring = after(ring, here)
    far = along_shift(ring, 1)
    ring, ring_rest = expert_rows(
        ((0, -1), (0, 1)), [ring, core_swap(ring)], *weights, cover=0.05
    )
    arrived_passed, far = tied(arrived_passed, far, ring)[:2]
    far, far_rest = expert_rows(
        ((2, 0), (2, 0)), [far, core_swap(far)], *weights, cover=0.05
    )
    far_sum = added(far, core_swap(far_rest)).astype(jnp.bfloat16)
    far_back = along_shift(far_sum, -1)
    passed = closed_up(arrived_passed, capacity)
    passed_other = core_swap(passed)
    passed, passed_rest = expert_rows(
        ((0, 1), (0, -1)), [after(passed, far_sum), passed_other], *weights, cover=0.05
    )
    ring_sum = added(ring, core_swap(ring_rest), after(far_back, passed)).astype(jnp.bfloat16)
    ring_back = along_shift(ring_sum, -1)
    sent_passed = padded(
        room, capacity, after(passed, ring_sum), core_swap(passed_rest)
    )
    returned_passed = lax.all_to_all(
        sent_passed.reshape(expert_count, room, width), "exp", 0, 0, tiled=True
    )
    sent = padded(room, capacity, here, core_swap(here_rest), ring_back)
    sent, returned_passed = tied(sent, returned_passed)
    returned = lax.all_to_all(
        sent.reshape(expert_count, room, width), "exp", 0, 0, tiled=True
    )
    (moe_passed,) = whole_call(
        weighed_rows, [((row_count, width), jnp.bfloat16)],
        returned_passed.reshape(expert_count * room, width), spread_passed,
        flops=4 * expert_count * room * row_count * width, moved=3 * MIB,
    )
    moe_passed = along_shift(moe_passed, 1)
    residual, root = whole_call(
        mixer_finish,
        [((row_count, width), jnp.bfloat16), ((row_count, 1), jnp.float32)],
        mixer_in[0], local, bc[0], grown, skip, shares, states_own, states_other,
        flops=2 * 6 * states * row_count * width, moved=6 * MIB,
    )
    resid_grad, adjoint = whole_call(
        norm_back,
        [whole, ((states, width), jnp.bfloat16)],
        returned.reshape(expert_count * room, width), spread, moe_passed, residual, root,
        norm_gain.astype(jnp.float32)[None, :], d_out[0], bc[0, :, states:].T, grown,
        flops=4 * expert_count * room * row_count * width, moved=6 * MIB,
    )
    (base,) = whole_call(
        back_local, [whole], resid_grad, back_weights, skip,
        flops=2 * 6 * 2 * row_count * row_count * width, moved=4 * MIB,
    )
    adjoints_own, adjoints_other = all_blocks(adjoint)
    (grad_in,) = whole_call(
        back_finish, [((row_count, width), jnp.bfloat16)],
        base, bc[0], to_end, shares_back, adjoints_own, adjoints_other,
        flops=2 * 6 * states * row_count * width, moved=4 * MIB,
    )
    return (residual[None], grad_in[None])


def solution(mesh):
    placed = (
        P("exp", "seq", None),
        P("exp", "seq", None),
        P("exp", "seq", None),
        P(),
        P(),
        P("exp", "seq", None),
        P("exp", "seq", None),
        P("exp", None, "seq"),
        P("exp", None, "seq"),
        P("exp", "seq", None),
        P("exp", None, None, "seq"),
        P("exp", "seq", None),
    )
    return jax.shard_map(
        per_device,
        mesh=mesh,
        in_specs=placed,
        out_specs=(P("exp", "seq", None), P("exp", "seq", None)),
        check_vma=False,
    )
```

```python
import functools

import jax
import jax.numpy as jnp
from jax import lax
from jax.experimental import pallas as pl
from jax.experimental.pallas import tpu as pltpu
from jax.sharding import PartitionSpec as P

HEAD = 64
PAIR = 2 * HEAD
STEP = 8
HIGHEST = lax.Precision.HIGHEST
EPSILON = 1e-05
MIB = 1024 * 1024
TILE = 1024
PARTS = 4
BY = (0, -1, 1, 2)


def chip_shift(value, by):
    chips = lax.axis_size("seq") // 2
    pairs = [(2 * z + c, 2 * ((z + by) % chips) + c) for z in range(chips) for c in range(2)]
    return lax.ppermute(value, "seq", pairs)


def core_swap(value):
    return lax.ppermute(value, "seq", [(i, i ^ 1) for i in range(lax.axis_size("seq"))])


def exact_dot(a, b, dims=((1,), (0,))):
    return lax.dot_general(
        a, b, (dims, ((), ())), precision=HIGHEST, preferred_element_type=jnp.float32
    )


def whole_call(body, outs, *args, flops=0, moved=0):
    vmem = pl.BlockSpec(memory_space=pltpu.VMEM)
    return pl.pallas_call(
        body,
        out_shape=[jax.ShapeDtypeStruct(shape, dtype) for shape, dtype in outs],
        in_specs=[vmem] * len(args),
        out_specs=[vmem] * len(outs),
        compiler_params=pltpu.CompilerParams(vmem_limit_bytes=32 * MIB),
        cost_estimate=pl.CostEstimate(flops=flops, bytes_accessed=moved, transcendentals=0),
    )(*args)


def added(*terms):
    total = terms[0].astype(jnp.float32)
    for term in terms[1:]:
        total = total + term.astype(jnp.float32)
    return total


def expert_kernel(places, *refs):
    count = steps = len(places)
    pieces, refs = refs[:count], refs[count:]
    saved, gate, up, down = refs[:4]
    outs, refs = refs[4 : 4 + count], refs[4 + count :]
    x, pre, w_gate, w_up, w_down, mixed, out, sem_x, sem_pre, sem_w, sem_out = refs
    part = pieces[0].shape[0]
    units, width = w_down.shape
    me = lax.axis_index("seq")
    chips = lax.axis_size("seq") // 2
    core = me % 2
    ahead = 1 - 2 * core

    def load(source, target, sem):
        rows = target.shape[0] // PARTS
        return [
            pltpu.make_async_copy(
                source.at[pl.ds(cut * rows, rows)], target.at[pl.ds(cut * rows, rows)], sem.at[cut]
            )
            for cut in range(PARTS)
        ]

    takes, befores, stores = [], [], []
    for piece, (away, along) in enumerate(places):
        chip = lax.rem(me // 2 + away + along * ahead + chips, chips)
        block = 2 * chip + (core if piece == 0 else 1 - core)
        start = pl.multiple_of(block * part, part)
        takes.append(load(pieces[piece], x.at[piece], sem_x.at[piece]))
        befores.append(
            [
                copy
                for kind in range(2)
                for copy in load(
                    saved.at[0, kind, pl.ds(start, part)], pre.at[piece, kind],
                    sem_pre.at[2 * piece + kind],
                )
            ]
        )
    cuts = [(low, min(low + 256, units)) for low in range(0, units, 256)]
    take_down = load(down, w_down, sem_w.at[0])
    take_rest = load(gate, w_gate, sem_w.at[1]) + load(up, w_up, sem_w.at[2])
    for copy in takes[0] + take_down + befores[0] + take_rest + takes[1] + befores[1]:
        copy.start()
    for step in range(steps):
        for copy in takes[step] + befores[step]:
            copy.wait()
        if step == 0:
            for copy in take_down:
                copy.wait()
        for low, high in cuts:
            hidden = lax.dot_general(
                x[step], w_down[low:high], (((1,), (1,)), ((), ())),
                preferred_element_type=jnp.float32,
            )
            gate_pre = pre[step, 0, :, low:high].astype(jnp.float32)
            up_pre = pre[step, 1, :, low:high].astype(jnp.float32)
            sigma = 0.5 * jnp.tanh(0.5 * gate_pre) + 0.5
            scaled = hidden * sigma
            mixed[step, :, low:high] = (scaled * up_pre * (1.0 + gate_pre * (1.0 - sigma))).astype(
                jnp.bfloat16
            )
            mixed[step, :, units + low : units + high] = (scaled * gate_pre).astype(jnp.bfloat16)
        if step == 0:
            for copy in take_rest:
                copy.wait()

        for low in range(0, width, TILE):
            weights = jnp.concatenate([w_gate[low : low + TILE], w_up[low : low + TILE]], axis=1)
            out[step, :, low : low + TILE] = lax.dot_general(
                mixed[step], weights, (((1,), (1,)), ((), ())),
                preferred_element_type=jnp.float32,
            ).astype(jnp.bfloat16)
            for half in range(2):
                store = pltpu.make_async_copy(
                    out.at[step, pl.ds(half * (part // 2), part // 2), pl.ds(low, TILE)],
                    outs[step].at[pl.ds(half * (part // 2), part // 2), pl.ds(low, TILE)],
                    sem_out.at[step, low // TILE, half],
                )
                store.start()
                stores.append(store)
    for store in stores:
        store.wait()


def expert_rows(places, pieces, saved, gate, up, down, cover=1.0):
    steps = count = len(pieces)
    rows = part = pieces[0].shape[0]
    units, width = down.shape
    anywhere = pl.BlockSpec(memory_space=pltpu.HBM)
    hbm = pl.BlockSpec(memory_space=pltpu.HBM)
    return pl.pallas_call(
        functools.partial(expert_kernel, places),
        out_shape=[jax.ShapeDtypeStruct((part, width), jnp.bfloat16)] * count,
        in_specs=[pl.BlockSpec(memory_space=pl.ANY)] * count + [hbm] * 4,
        out_specs=[anywhere] * count,
        scratch_shapes=[
            pltpu.VMEM((steps, rows, width), jnp.bfloat16),
            pltpu.VMEM((steps, 2, rows, units), jnp.bfloat16),
            pltpu.VMEM((width, units), jnp.bfloat16),
            pltpu.VMEM((width, units), jnp.bfloat16),
            pltpu.VMEM((units, width), jnp.bfloat16),
            pltpu.VMEM((steps, rows, 2 * units), jnp.bfloat16),
            pltpu.VMEM((steps, rows, width), jnp.bfloat16),
            pltpu.SemaphoreType.DMA((count, PARTS)),
            pltpu.SemaphoreType.DMA((2 * count, PARTS)),
            pltpu.SemaphoreType.DMA((3, PARTS)),
            pltpu.SemaphoreType.DMA((count, width // TILE, 2)),
        ],
        compiler_params=pltpu.CompilerParams(vmem_limit_bytes=60 * MIB),
        cost_estimate=pl.CostEstimate(
            flops=int(cover * 6 * count * part * units * width),
            bytes_accessed=int(cover * 6 * units * width),
            transcendentals=0,
        ),
    )(*pieces, saved, gate, up, down)


def mixer_local(x, bc, write_t, cum, cum_t, local, back_weights, state, grown, to_end):
    rows, width = x.shape
    heads = cum.shape[1]
    states = write_t.shape[0]
    write, read = bc[:, :states], bc[:, states:]
    dims = (((1,), (1,)), ((), ()))
    scores = lax.dot_general(read, write, dims, preferred_element_type=jnp.float32)
    scores_t = lax.dot_general(write, read, dims, preferred_element_type=jnp.float32)
    row = lax.broadcasted_iota(jnp.int32, (rows, rows), 0)
    col = lax.broadcasted_iota(jnp.int32, (rows, rows), 1)
    low_lanes = lax.broadcasted_iota(jnp.int32, (rows, PAIR), 1) < HEAD
    for pair in range(heads // 2):
        at = pair * PAIR
        values = x[:, at : at + PAIR].astype(jnp.float32)
        parts = []
        for head in (2 * pair, 2 * pair + 1):
            gap = cum[:, head : head + 1] - cum_t[head : head + 1, :]
            weights = jnp.where(row >= col, jnp.exp(jnp.minimum(gap, 0.0)), 0.0) * scores
            back_weights[head] = (
                jnp.where(col >= row, jnp.exp(jnp.minimum(-gap, 0.0)), 0.0) * scores_t
            )
            parts.append(exact_dot(weights, values))
        local[:, at : at + PAIR] = jnp.where(low_lanes, parts[0], parts[1])
    own = lax.broadcasted_iota(jnp.int32, (heads, width), 1) // HEAD
    spread = (own == lax.broadcasted_iota(jnp.int32, (heads, width), 0)).astype(jnp.float32)
    last = cum[rows - 1 : rows, :]
    grown[...] = exact_dot(jnp.exp(cum[...]), spread)
    ends = exact_dot(jnp.exp(last - cum[...]), spread)
    to_end[...] = ends
    added_state = exact_dot(write_t[...].astype(jnp.float32), ends * x[...].astype(jnp.float32))
    state[:states, :] = added_state.astype(jnp.bfloat16)
    sums = exact_dot(jnp.broadcast_to(last, (states, heads)), spread)
    term = lax.broadcasted_iota(jnp.int32, (states, width), 0)
    high = sums.astype(jnp.bfloat16).astype(jnp.float32)
    middle = (sums - high).astype(jnp.bfloat16).astype(jnp.float32)
    low = sums - high - middle
    terms = jnp.where(term == 0, high, jnp.where(term == 1, middle, jnp.where(term == 2, low, 0.0)))
    state[states:, :] = terms.astype(jnp.bfloat16)


def mixer_finish(x, local, bc, grown, skip, shares, states_own, states_other, residual, root):
    states = bc.shape[1] // 2
    blocks = states_own.shape[0]
    incoming = jnp.zeros((states, x.shape[1]), jnp.float32)
    for block in range(blocks):
        incoming += shares[block : block + 1, :] * states_own[block, :states].astype(jnp.float32)
        incoming += shares[blocks + block : blocks + block + 1, :] * states_other[block, :states].astype(jnp.float32)
    carried = exact_dot(bc[:, states:].astype(jnp.float32), incoming)
    values = x[...].astype(jnp.float32)
    total = values + (local[...] + grown[...] * carried + skip[...] * values)
    rounded = total.astype(jnp.bfloat16)
    residual[...] = rounded
    again = rounded.astype(jnp.float32)
    root[...] = jnp.sqrt(jnp.mean(again * again, axis=-1, keepdims=True) + EPSILON)


def weighed(weights, rows):
    count = weights.shape[0]
    high = weights.astype(jnp.bfloat16)
    rest = (weights - high.astype(jnp.float32)).astype(jnp.bfloat16)
    both = lax.dot_general(
        jnp.concatenate([high, rest], axis=0), rows, (((1,), (0,)), ((), ())),
        preferred_element_type=jnp.float32,
    )
    return both[:count] + both[count:]


def weighed_rows(returned, spread, out):
    out[...] = weighed(spread[...], returned[...]).astype(jnp.bfloat16)


def padded_sum(room, capacity, *refs):
    terms, out = refs[:-1], refs[-1]
    total = terms[0][...].astype(jnp.float32)
    for term in terms[1:]:
        total = total + term[...].astype(jnp.float32)
    place = lax.broadcasted_iota(jnp.int32, (out.shape[0], total.shape[0]), 0)
    row = lax.broadcasted_iota(jnp.int32, (out.shape[0], total.shape[0]), 1)
    slot = place % room
    opened = ((slot < capacity) & (row == (place // room) * capacity + slot)).astype(jnp.float32)
    out[...] = lax.dot_general(
        opened.astype(jnp.bfloat16), total.astype(jnp.bfloat16), (((1,), (0,)), ((), ())),
        preferred_element_type=jnp.float32,
    ).astype(jnp.bfloat16)


def padded(room, capacity, *terms):
    rows, width = terms[0].shape
    count = rows // capacity * room
    tile = 512
    return pl.pallas_call(
        functools.partial(padded_sum, room, capacity),
        out_shape=jax.ShapeDtypeStruct((count, width), jnp.bfloat16),
        grid=(width // tile,),
        in_specs=[pl.BlockSpec((rows, tile), lambda i: (0, i))] * len(terms),
        out_specs=pl.BlockSpec((count, tile), lambda i: (0, i)),
        compiler_params=pltpu.CompilerParams(vmem_limit_bytes=24 * MIB),
        cost_estimate=pl.CostEstimate(
            flops=2 * rows * count * width, bytes_accessed=2 * (len(terms) + 1) * rows * width,
            transcendentals=0,
        ),
    )(*terms)


def norm_back(returned, spread, passed, residual, root, gain, d_out, read_t, grown, resid_grad, adjoint):
    moe_grad = weighed(spread[...], returned[...]) + passed[...].astype(jnp.float32)
    scaled = moe_grad * gain[...]
    normed = residual[...].astype(jnp.float32) / root[...]
    along = jnp.mean(scaled * normed, axis=-1, keepdims=True)
    gradient = d_out[...].astype(jnp.float32) + (scaled - normed * along) / root[...]
    resid_grad[...] = gradient
    adjoint[...] = exact_dot(read_t[...].astype(jnp.float32), grown[...] * gradient).astype(
        jnp.bfloat16
    )


def back_local(resid_grad, back_weights, skip, base):
    rows = resid_grad.shape[0]
    low_lanes = lax.broadcasted_iota(jnp.int32, (rows, PAIR), 1) < HEAD
    for pair in range(back_weights.shape[0] // 2):
        at = pair * PAIR
        gradient = resid_grad[:, at : at + PAIR]
        first = exact_dot(back_weights[2 * pair], gradient)
        second = exact_dot(back_weights[2 * pair + 1], gradient)
        mixed = jnp.where(low_lanes, first, second)
        base[:, at : at + PAIR] = gradient + (mixed + skip[:, at : at + PAIR] * gradient)


def back_finish(base, bc, to_end, shares, own, other, grad_in):
    states = bc.shape[1] // 2
    blocks = own.shape[0]
    after = jnp.zeros((states, base.shape[1]), jnp.float32)
    for block in range(blocks):
        after += shares[block : block + 1, :] * own[block].astype(jnp.float32)
        after += shares[blocks + block : blocks + block + 1, :] * other[block].astype(jnp.float32)
    carried = exact_dot(bc[:, :states].astype(jnp.float32), after)
    grad_in[...] = (base[...] + to_end[...] * carried).astype(jnp.bfloat16)


def block_ids():
    me = lax.axis_index("seq")
    chips = lax.axis_size("seq") // 2
    z, core = me // 2, me % 2
    there = [2 * ((z + by) % chips) for by in BY]
    return jnp.stack([t + core for t in there] + [t + 1 - core for t in there]).astype(jnp.int32)


def all_blocks(value, *earlier):
    own = jnp.stack([value] + [chip_shift(value, -by) for by in BY[1:]])
    own = after(own, *earlier)
    return own, core_swap(own)


def shares_of(ids, log_sums, backwards):
    me = lax.axis_index("seq")
    place = -ids if backwards else ids
    here = -me if backwards else me
    crossed = (place[None, :] > place[:, None]) & (place[None, :] < here)
    exponent = jnp.sum(jnp.where(crossed[:, :, None], log_sums[None], 0.0), axis=1)
    return jnp.where((place < here)[:, None], jnp.exp(exponent), 0.0)


def tied(*values):
    return lax.optimization_barrier(values)


def after(value, *others):
    return lax.optimization_barrier((value, *others))[0]


def along_shift(value, by):
    chips = lax.axis_size("seq") // 2
    pairs = [
        (2 * z + c, 2 * ((z + by * (1 - 2 * c)) % chips) + c) for z in range(chips) for c in range(2)
    ]
    return lax.ppermute(value, "seq", pairs)


def close_up(room, capacity, arrived, out):
    parts = 2
    count, rows = out.shape[0] // parts, arrived.shape[0] // parts
    place = lax.broadcasted_iota(jnp.int32, (count, rows), 0)
    row = lax.broadcasted_iota(jnp.int32, (count, rows), 1)
    kept = row == (place // capacity) * room + place % capacity
    kept = kept.astype(jnp.float32).astype(jnp.bfloat16)
    for part in range(parts):
        out[part * count : (part + 1) * count] = lax.dot_general(
            kept, arrived[part * rows : (part + 1) * rows], (((1,), (0,)), ((), ())),
            preferred_element_type=jnp.float32,
        ).astype(jnp.bfloat16)


def closed_up(arrived, capacity):
    experts, room, width = arrived.shape
    tile = 512
    count = experts * capacity
    return pl.pallas_call(
        functools.partial(close_up, room, capacity),
        out_shape=jax.ShapeDtypeStruct((count, width), jnp.bfloat16),
        grid=(width // tile,),
        in_specs=[pl.BlockSpec((experts * room, tile), lambda i: (0, i))],
        out_specs=pl.BlockSpec((count, tile), lambda i: (0, i)),
        compiler_params=pltpu.CompilerParams(vmem_limit_bytes=24 * MIB),
        cost_estimate=pl.CostEstimate(
            flops=experts * room * count * width, bytes_accessed=4 * count * width,
            transcendentals=0,
        ),
    )(arrived.reshape(experts * room, width))


def per_device(
    mixer_in,
    bc,
    log_decay,
    skip_gain,
    norm_gain,
    routes,
    route_weight,
    w_gate,
    w_up,
    w_down,
    saved_pre,
    d_out,
):
    row_count = mixer_in.shape[1]
    width = mixer_in.shape[2]
    heads = log_decay.shape[2]
    states = bc.shape[2] // 2
    expert_count = lax.axis_size("exp")
    capacity = saved_pre.shape[2] // (lax.axis_size("seq") * expert_count)
    room = -(-capacity // STEP) * STEP
    per_token = routes.shape[2]
    whole, table = ((row_count, width), jnp.float32), ((heads, row_count, row_count), jnp.float32)
    ids = block_ids()

    chosen = routes[0].reshape(row_count * per_token)
    onehot = (chosen[:, None] == jnp.arange(expert_count, dtype=jnp.int32)[None, :]).astype(
        jnp.int32
    )
    earlier = jnp.cumsum(onehot, axis=0) - onehot
    slot_index = jnp.sum(earlier * onehot, axis=1)
    target = (chosen * room + slot_index).reshape(row_count, per_token)
    places = jnp.arange(expert_count * room, dtype=jnp.int32)
    notes = jnp.concatenate([target.astype(jnp.float32), route_weight[0]], axis=1)

    def slotted(target, weight, rows):
        hit = target[:, :, None] == places[None, None, :]
        spread = jnp.sum(jnp.where(hit, weight[:, :, None], 0.0), axis=1)
        picked = jnp.any(hit, axis=1).T.astype(jnp.bfloat16)
        packed = jnp.dot(picked, rows, preferred_element_type=jnp.float32).astype(jnp.bfloat16)
        return spread, packed.reshape(expert_count, room, width)

    spread, packed = slotted(target, route_weight[0], d_out[0])
    d_out_passed = along_shift(after(d_out[0], packed), -1)
    notes_passed = along_shift(notes, -1)
    spread_passed, packed_passed = slotted(
        notes_passed[:, :per_token].astype(jnp.int32), notes_passed[:, per_token:], d_out_passed
    )

    arrived = lax.all_to_all(packed, "exp", 0, 0, tiled=True)
    log_rates = after(log_decay[0], packed)

    cum = jnp.cumsum(log_rates, axis=0)
    skip = jnp.repeat(skip_gain, HEAD)[None, :]
    local, back_weights, state, grown, to_end = whole_call(
        mixer_local,
        [whole, table, ((2 * states, width), jnp.bfloat16), whole, whole],
        mixer_in[0], bc[0], bc[0, :, :states].T, cum, cum.T,
        flops=2 * 6 * 2 * row_count * row_count * width, moved=8 * MIB,
    )
    states_own, states_other = all_blocks(state, d_out_passed)
    log_sums = jnp.concatenate([states_own[:, states:], states_other[:, states:]])
    log_sums = jnp.sum(log_sums.astype(jnp.float32), axis=1)
    arrived, states_own, states_other, log_sums = tied(arrived, states_own, states_other, log_sums)
    arrived = after(arrived, d_out_passed, notes_passed)
    packed_passed = after(packed_passed, arrived)
    shares = shares_of(ids, log_sums, False)
    shares_back = shares_of(ids, log_sums, True)
    weights = (saved_pre, w_gate[0], w_up[0], w_down[0])
    rows = closed_up(arrived, capacity)
    ring = along_shift(rows, 1)
    arrived_passed = lax.all_to_all(packed_passed, "exp", 0, 0, tiled=True)
    here, here_rest = expert_rows(((0, 0), (0, 0)), [rows, core_swap(rows)], *weights)
    ring = after(ring, here)
    far = along_shift(ring, 1)
    ring, ring_rest = expert_rows(
        ((0, -1), (0, 1)), [ring, core_swap(ring)], *weights, cover=0.05
    )
    arrived_passed, far = tied(arrived_passed, far, ring)[:2]
    far, far_rest = expert_rows(
        ((2, 0), (2, 0)), [far, core_swap(far)], *weights, cover=0.05
    )
    far_sum = added(far, core_swap(far_rest)).astype(jnp.bfloat16)
    far_back = along_shift(far_sum, -1)
    passed = closed_up(arrived_passed, capacity)
    passed_other = core_swap(passed)
    passed, passed_rest = expert_rows(
        ((0, 1), (0, -1)), [after(passed, far_sum), passed_other], *weights, cover=0.05
    )
    ring_sum = added(ring, core_swap(ring_rest), after(far_back, passed)).astype(jnp.bfloat16)
    ring_back = along_shift(ring_sum, -1)
    sent_passed = padded(
        room, capacity, after(passed, ring_sum), core_swap(passed_rest)
    )
    returned_passed = lax.all_to_all(
        sent_passed.reshape(expert_count, room, width), "exp", 0, 0, tiled=True
    )
    sent = padded(room, capacity, here, core_swap(here_rest), ring_back)
    sent, returned_passed = tied(sent, returned_passed)
    returned = lax.all_to_all(
        sent.reshape(expert_count, room, width), "exp", 0, 0, tiled=True
    )
    (moe_passed,) = whole_call(
        weighed_rows, [((row_count, width), jnp.bfloat16)],
        returned_passed.reshape(expert_count * room, width), spread_passed,
        flops=4 * expert_count * room * row_count * width, moved=3 * MIB,
    )
    moe_passed = along_shift(moe_passed, 1)
    residual, root = whole_call(
        mixer_finish,
        [((row_count, width), jnp.bfloat16), ((row_count, 1), jnp.float32)],
        mixer_in[0], local, bc[0], grown, skip, shares, states_own, states_other,
        flops=2 * 6 * states * row_count * width, moved=6 * MIB,
    )
    resid_grad, adjoint = whole_call(
        norm_back,
        [whole, ((states, width), jnp.bfloat16)],
        returned.reshape(expert_count * room, width), spread, moe_passed, residual, root,
        norm_gain.astype(jnp.float32)[None, :], d_out[0], bc[0, :, states:].T, grown,
        flops=4 * expert_count * room * row_count * width, moved=6 * MIB,
    )
    (base,) = whole_call(
        back_local, [whole], resid_grad, back_weights, skip,
        flops=2 * 6 * 2 * row_count * row_count * width, moved=4 * MIB,
    )
    adjoints_own, adjoints_other = all_blocks(adjoint)
    (grad_in,) = whole_call(
        back_finish, [((row_count, width), jnp.bfloat16)],
        base, bc[0], to_end, shares_back, adjoints_own, adjoints_other,
        flops=2 * 6 * states * row_count * width, moved=4 * MIB,
    )
    return (residual[None], grad_in[None])


def solution(mesh):
    placed = (
        P("exp", "seq", None),
        P("exp", "seq", None),
        P("exp", "seq", None),
        P(),
        P(),
        P("exp", "seq", None),
        P("exp", "seq", None),
        P("exp", None, "seq"),
        P("exp", None, "seq"),
        P("exp", "seq", None),
        P("exp", None, None, "seq"),
        P("exp", "seq", None),
    )
    return jax.shard_map(
        per_device,
        mesh=mesh,
        in_specs=placed,
        out_specs=(P("exp", "seq", None), P("exp", "seq", None)),
        check_vma=False,
    )
```
